128 devices in a mesh: dp: 4 (over y_hi, core), fsdp: 32 (over z, y_lo, x).
Axes of the slice: x: 4, y: 4 (y_hi: 2, y_lo: 2; y = y_hi * 2 + y_lo), z: 4, core: 2. Of those that a mesh axis runs over, the one named last changes fastest.
Arguments:
- tokens: bfloat16 [2, 65536, 768], P(None, ('dp', 'fsdp')), may hold values from -6 to 6
- parts: int32 [2, 128, 8], P(None, ('dp', 'fsdp')), may hold values from 1 to 128, 512 in all within a row
- cotangent: bfloat16 [2, 65536, 768], P(None, ('dp', 'fsdp'))
- w_query: bfloat16 [768, 768], P(('dp', 'fsdp')), may hold values from -0.21875 to 0.21875
- w_key: bfloat16 [768, 768], P(('dp', 'fsdp')), may hold values from -0.21875 to 0.21875
- w_value: bfloat16 [768, 768], P(('dp', 'fsdp')), may hold values from -0.21875 to 0.21875
- w_out: bfloat16 [768, 768], P(('dp', 'fsdp')), may hold values from -0.625 to 0.625
- w_up: bfloat16 [768, 3072], P(('dp', 'fsdp')), may hold values from -0.21875 to 0.21875
- w_down: bfloat16 [3072, 768], P(('dp', 'fsdp')), may hold values from -0.109375 to 0.109375
- shared_a: bfloat16 [768, 1024], P(('dp', 'fsdp')), may hold values from -0.21875 to 0.21875
- shared_b: bfloat16 [1024, 768], P(('dp', 'fsdp')), may hold values from -0.1875 to 0.1875
- gain_one: float32 [768], replicated, may hold values from 0.1 to 1.9
- shift_one: float32 [768], replicated, may hold values from -1.5 to 1.5
- gain_two: float32 [768], replicated, may hold values from 0.1 to 1.9
- shift_two: float32 [768], replicated, may hold values from -1.5 to 1.5
- scale_dq: float32 [1024], replicated, may hold values from 0.3 to 1.5
- scale_bq: float32 [768], replicated, may hold values from -2.5 to 2.5
- scale_dv: float32 [1024], replicated, may hold values from 0.3 to 1.5
- scale_bv: float32 [768], replicated, may hold values from -2.5 to 2.5
Outputs:
- output: bfloat16 [2, 65536, 768], P(None, ('dp', 'fsdp'))
- grad_tokens: bfloat16 [2, 65536, 768], P(None, ('dp', 'fsdp'))
- grad_dq: float32 [1024], replicated
- grad_bq: float32 [768], replicated
- grad_dv: float32 [1024], replicated
- grad_bv: float32 [768], replicated
The draws below stay inside these ranges and needn't reach their ends.
Inputs may be any that keep to these rules, and one draw needn't show every extreme that they name: `parts`: in every packed row the 4 pairs' two sentence lengths fill the row's 512 tokens exactly; entries 2p and 2p+1 are pair p's first and second sentence.
All inputs are finite; a program needn't handle non-finite values.
Results may differ from the reference program's by a relative error of at most 0.014.
Values may be sent and summed in bfloat16 or wider, within the bound.
A program may use at most 256 MiB of HBM per device.

```python
import math
import jax
import jax.numpy as jnp
import numpy as np
from jax import lax

D = 768
HEADS = 12
HEAD_DIM = 64
FF = 3072
RANK = 1024
TOK_DEV = 512
MICRO = 2
PAIRS = 4
TOKENS = 65536
DEVICES = 128


def draw_cotangent(key, part):
    key = jax.random.fold_in(key, 11)
    spread_pos = jnp.arange(TOKENS, dtype=jnp.float32) / TOKENS
    row_scale = (0.5 + spread_pos)[None, :, None]
    normal_part = jax.random.normal(key, (MICRO, TOKENS, D), jnp.float32)
    return (normal_part * row_scale).astype(jnp.bfloat16)


def block_levels(key, extent, shards, low, top_value):
    gain = 1.0
    for dim, shards_of in shards:
        steps = jax.random.uniform(jax.random.fold_in(jax.random.fold_in(key, 6), dim), (shards_of,), jnp.float32, low / len(shards), top_value / len(shards))
        gain = gain * jnp.repeat(jnp.exp(steps), extent[dim] // shards_of).reshape((-1,) + (1,) * (len(extent) - 1 - dim))
    return gain


def split_up(count, total, limit, skew):
    loads = [(1 << 20) // math.isqrt(standing ** skew) + 1 for standing in range(2, count + 1)]
    surplus, holding = total - limit - (count - 1), [1] * (count - 1)
    while surplus > 0:
        movable = [i for i in range(count - 1) if holding[i] < limit]
        whole, left = sum([loads[i] for i in movable]), surplus
        for i in movable:
            addition = min(limit - holding[i], max(1, left * loads[i] // whole), surplus)
            holding[i] = holding[i] + addition
            surplus = surplus - addition
    return np.array([limit] + holding)


def ragged(key, count, total, most, lean):
    if count == 2:
        one = jax.random.randint(key, (), max(1, total - most), min(most, total - 1) + 1)
        return jnp.stack([one, total - one])
    tallies = jnp.asarray(split_up(count, total, most, lean), jnp.int32)
    twos = (count - 1) // 2
    donor, receiver = tallies[1:1 + 2 * twos:2], tallies[2:2 + 2 * twos:2]
    margin = jnp.minimum(donor - 1, most - receiver)
    passed = jax.random.randint(jax.random.fold_in(key, 1), (twos,), 0, 1 << 20) % (margin + 1)
    tallies = tallies.at[1:1 + 2 * twos:2].set(donor - passed).at[2:2 + 2 * twos:2].set(receiver + passed)
    return tallies[jax.random.permutation(jax.random.fold_in(key, 2), count)]


def normal_values(rng, dims, scale, limit, shards=(), kind=jnp.bfloat16):
    values = scale * jax.random.normal(rng, dims, jnp.float32)
    if shards:
        values = values * block_levels(rng, dims, shards, -0.22, 0.18)
    return jnp.clip(values, -limit, limit).astype(kind)


def setup_inputs(seed: int = 0) -> dict:
    keys = jax.random.split(jax.random.key(seed), 20)
    tokens = normal_values(keys[0], (MICRO, TOKENS, D), 1.0, 6.0, ((1, 128),))
    parts = jax.vmap(lambda own: ragged(own, 2 * PAIRS, TOK_DEV, TOK_DEV // 4, 1))(jax.random.split(keys[1], MICRO * DEVICES)).reshape((MICRO, DEVICES, 2 * PAIRS)).astype(jnp.int32)
    cotangent = draw_cotangent(jax.random.fold_in(keys[19], 71), 0)
    w_query = normal_values(keys[3], (D, D), D ** -0.5, 0.21875, ((0, 128),))
    w_key = normal_values(keys[4], (D, D), D ** -0.5, 0.21875, ((0, 128),))
    w_value = normal_values(keys[5], (D, D), D ** -0.5, 0.21875, ((0, 128),))
    w_out = normal_values(keys[6], (D, D), (D // 8) ** -0.5, 0.625, ((0, 128),))
    w_up = normal_values(keys[7], (D, FF), D ** -0.5, 0.21875, ((0, 128),))
    w_down = normal_values(keys[8], (FF, D), FF ** -0.5, 0.109375, ((0, 128),))
    shared_a = normal_values(keys[9], (D, RANK), D ** -0.5, 0.21875, ((0, 128),))
    shared_b = normal_values(keys[10], (RANK, D), RANK ** -0.5, 0.1875, ((0, 128),))
    gain_one = jnp.clip(1.0 + 0.18 * jax.random.normal(keys[11], (D,), jnp.float32), 0.1, 1.9)
    shift_one = normal_values(keys[12], (D,), 0.3, 1.5, (), jnp.float32)
    gain_two = jnp.clip(1.0 + 0.18 * jax.random.normal(keys[13], (D,), jnp.float32), 0.1, 1.9)
    shift_two = normal_values(keys[14], (D,), 0.3, 1.5, (), jnp.float32)
    scale_dq = jnp.clip(jnp.exp(jax.random.uniform(keys[15], (RANK,), jnp.float32, math.log(0.3), math.log(1.5))), 0.3, 1.5)
    scale_bq = normal_values(keys[16], (D,), 0.5, 2.5, (), jnp.float32)
    scale_dv = jnp.clip(jnp.exp(jax.random.uniform(keys[17], (RANK,), jnp.float32, math.log(0.3), math.log(1.5))), 0.3, 1.5)
    scale_bv = normal_values(keys[18], (D,), 0.5, 2.5, (), jnp.float32)
    return dict(tokens=tokens, parts=parts, cotangent=cotangent, w_query=w_query, w_key=w_key, w_value=w_value, w_out=w_out, w_up=w_up, w_down=w_down, shared_a=shared_a, shared_b=shared_b, gain_one=gain_one, shift_one=shift_one, gain_two=gain_two, shift_two=shift_two, scale_dq=scale_dq, scale_bq=scale_bq, scale_dv=scale_dv, scale_bv=scale_bv)


@jax.custom_vjp
def low(v):
    return lax.optimization_barrier(v.astype(jnp.bfloat16)).astype(jnp.float32)

@jax.custom_vjp
def low_back(v):
    return v

def low_keep(v):
    return (low(v), None)

def low_pass(kept, grad):
    return (grad,)

def back_keep(v):
    return (v, None)

def back_low(kept, grad):
    return (low(grad),)
low.defvjp(low_keep, low_pass)
low_back.defvjp(back_keep, back_low)
exact_prec = lax.Precision.HIGHEST

def matmul(left, right):
    return jnp.matmul(left, right, precision=exact_prec)

def norm_layer(stream, gain_vec, shift_vec):
    average = lax.optimization_barrier(jnp.mean(stream, axis=-1, keepdims=True))
    centred = stream - average
    variance = lax.optimization_barrier(jnp.mean(centred * centred, axis=-1, keepdims=True))
    return centred * lax.rsqrt(variance + 1e-05) * gain_vec + shift_vec

def pair_mask(lengths, width):
    pair_sizes = lengths[:, 0::2] + lengths[:, 1::2]
    pair_ends = jnp.cumsum(pair_sizes, axis=-1)
    position = jnp.arange(width, dtype=jnp.int32)
    pair_id = lax.optimization_barrier(jnp.sum((position[None, :, None] >= pair_ends[:, None, :]).astype(jnp.int32), axis=-1))
    return pair_id[:, :, None] == pair_id[:, None, :]

def encoder(stream, allowed, weights, vectors, norms):
    w_query, w_key, w_value, w_out, w_up, w_down, shared_a, shared_b = weights
    scale_dq, scale_bq, scale_dv, scale_bv = vectors
    gain_one, shift_one, gain_two, shift_two = norms
    groups, length = (stream.shape[0], stream.shape[1])
    lowered = low(stream)
    latent = low_back(matmul(lowered, shared_a))
    query_u = low(latent * scale_dq)
    value_u = low(latent * scale_dv)
    query_rows = low(low_back(matmul(lowered, w_query) + scale_bq * low_back(matmul(query_u, shared_b))))
    key_rows = low(low_back(matmul(lowered, w_key)))
    value_rows = low(low_back(matmul(lowered, w_value) + scale_bv * low_back(matmul(value_u, shared_b))))
    query_heads = query_rows.reshape(groups, length, HEADS, HEAD_DIM)
    key_heads = key_rows.reshape(groups, length, HEADS, HEAD_DIM)
    value_heads = value_rows.reshape(groups, length, HEADS, HEAD_DIM)
    logits = jnp.einsum('glhe,gmhe->ghlm', query_heads, key_heads, precision=exact_prec) * (1.0 / math.sqrt(HEAD_DIM))
    scores = low_back(jnp.where(allowed[:, None], logits, -1e+30))
    softmaxed = jax.nn.softmax(scores, axis=-1)
    mixed = jnp.einsum('ghlm,gmhe->glhe', low(softmaxed), value_heads, precision=exact_prec).reshape(groups, length, D)
    attended = low(low_back(mixed))
    first = norm_layer(stream + low_back(matmul(attended, w_out)), gain_one, shift_one)
    upper = low_back(matmul(low(first), w_up))
    hidden = low(jax.nn.gelu(upper, approximate=False))
    return norm_layer(first + low_back(matmul(hidden, w_down)), gain_two, shift_two)

def reference(tokens, parts, cotangent, w_query, w_key, w_value, w_out, w_up, w_down, shared_a, shared_b, gain_one, shift_one, gain_two, shift_two, scale_dq, scale_bq, scale_dv, scale_bv):
    width = tokens.shape[2]
    total_rows = tokens.shape[0] * tokens.shape[1] // TOK_DEV
    group_rows = math.gcd(8, total_rows)
    count = total_rows // group_rows
    stream = tokens.astype(jnp.float32).reshape(count, group_rows, TOK_DEV, width)
    cots = cotangent.astype(jnp.float32).reshape(count, group_rows, TOK_DEV, width)
    lengths = parts.reshape(count, group_rows, parts.shape[2])
    weights = tuple((matrix.astype(jnp.float32) for matrix in (w_query, w_key, w_value, w_out, w_up, w_down, shared_a, shared_b)))
    vectors = (scale_dq, scale_bq, scale_dv, scale_bv)
    norms = (gain_one, shift_one, gain_two, shift_two)

    def scan_step(running, pieces):
        rows_now, cots_now, lengths_now = pieces
        allowed = pair_mask(lengths_now, TOK_DEV)

        def forward(rows_in, vector_in):
            return encoder(rows_in, allowed, weights, vector_in, norms)
        result, pullback = jax.vjp(forward, rows_now, vectors)
        grad_rows, grad_vectors = pullback(cots_now)
        running = tuple((left + right for left, right in zip(running, grad_vectors)))
        return (running, (result, grad_rows))
    start = tuple((jnp.zeros_like(vector) for vector in vectors))
    sums, (results, grads) = lax.scan(scan_step, start, (stream, cots, lengths))
    output = results.reshape(tokens.shape).astype(jnp.bfloat16)
    grad_tokens = grads.reshape(tokens.shape).astype(jnp.bfloat16)
    return (output, grad_tokens, sums[0], sums[1], sums[2], sums[3])
```

```python
import jax
import jax.numpy as jnp
from jax import lax
from jax.experimental import pallas as pl
from jax.experimental.pallas import tpu as pltpu
from jax.sharding import PartitionSpec as P

MESH = pl.DeviceIdType.MESH
BF = jnp.bfloat16
F32 = jnp.float32


def place():
    dp = lax.axis_index("dp")
    fs = lax.axis_index("fsdp")
    return dict(x=fs % 4, y=(dp // 2) * 2 + (fs // 4) % 2, z=fs // 8, c=dp % 2)


def device(at):
    return ((at["y"] // 2) * 2 + at["c"], at["z"] * 8 + (at["y"] % 2) * 4 + at["x"])


def moved(at, axis, delta):
    size = 2 if axis == "c" else 4
    return {**at, axis: (at[axis] + delta + size) % size}


ORDERS = (("x", "y", "z"), ("y", "z", "x"), ("z", "x", "y"))
PEERS = 13


def peers(at):
    found = []
    for dx in range(4):
        for dy in range(2):
            if dx or dy:
                found.append({**at, "x": (at["x"] + dx) % 4, "y": (at["y"] // 2) * 2 + (at["y"] + dy) % 2})
    for dy in range(2):
        found.append({**at, "y": (1 - at["y"] // 2) * 2 + dy})
    for delta in range(1, 4):
        found.append(moved(at, "z", delta))
    found.append(moved(at, "c", 1))
    return found


def enter_signal(at):
    for peer in peers(at):
        pl.semaphore_signal(pltpu.get_barrier_semaphore(), inc=1, device_id=device(peer), device_id_type=MESH)


def region(buf, kind, rot, done, at, low, high):
    every = slice(None)
    x, y, z, c = at["x"], at["y"], at["z"], at["c"]
    yh = every if "y" in done else y // 2
    yl = every if "y" in done else y % 2
    zs = every if "z" in done else z
    if kind == "panel":
        col = every if "x" in done else pl.ds(pl.multiple_of(x * 128, 128), 128)
        return buf.at[low:high, yl, yh, c, zs, rot, :, col]
    col = every if "x" in done else pl.ds(pl.multiple_of((x % 2) * 384, 128), 384)
    half = every if "x" in done else x // 2
    if kind == "down":
        return buf.at[yh, c, zs, yl, half, rot, :, col]
    return buf.at[yh, c, zs, yl, half, :, col]


class Moves:
    def __init__(self, at, bufs, send, recv):
        self.at, self.bufs, self.send, self.recv = at, bufs, send, recv
        self.slots = {}

    def slot(self, key):
        return self.slots.setdefault(key, len(self.slots))

    def copies(self, group, phase):
        kind, low, high = group
        buf = self.bufs[kind]
        for rot in (1,) if kind == "up_b" else range(3):
            order = ORDERS[rot]
            axis, done = order[phase], order[:phase]
            for delta in (1, 3, 2):
                k = self.slot((group, phase, rot, delta))
                yield (
                    region(buf, kind, rot, done, self.at, low, high),
                    moved(self.at, axis, delta),
                    region(buf, kind, rot, done, moved(self.at, axis, -delta), low, high),
                    k,
                )

    def sibling(self, group):
        kind, low, high = group
        buf = self.bufs[kind]
        k = self.slot((group, "c"))
        for here in (self.at,):
            other = moved(here, "c", 1)
            if kind == "panel":
                mine, theirs = buf.at[low:high, :, :, here["c"]], buf.at[low:high, :, :, other["c"]]
            else:
                mine, theirs = buf.at[:, here["c"]], buf.at[:, other["c"]]
            yield mine, other, theirs, k

    def make(self, what):
        mine, target, theirs, k = what
        return pltpu.make_async_remote_copy(
            src_ref=mine,
            dst_ref=mine,
            send_sem=self.send.at[k],
            recv_sem=self.recv.at[k],
            device_id=device(target),
            device_id_type=MESH,
        )

    def arrival(self, what):
        mine, target, theirs, k = what
        return pltpu.make_async_remote_copy(
            src_ref=theirs,
            dst_ref=theirs,
            send_sem=self.send.at[k],
            recv_sem=self.recv.at[k],
            device_id=device(target),
            device_id_type=MESH,
        )

    def listed(self, group, phase):
        return self.sibling(group) if phase == 3 else self.copies(group, phase)

    def start(self, group, phase):
        for what in self.listed(group, phase):
            self.make(what).start()

    def wait(self, group, phase):
        for what in self.listed(group, phase):
            self.arrival(what).wait_recv()

    def sent(self, group, phase):
        for what in self.listed(group, phase):
            self.make(what).wait_send()


def stage_zero(at, shards, packed, landed, half_d, half_b, rows, bufs, send, recv):
    w_query, w_key, w_value, w_out, w_up, w_down, shared_a, shared_b = shards
    kvqo = (w_key, w_value, w_query, w_out)
    x, y, z, c = at["x"], at["y"], at["z"], at["c"]
    mine = (y % 2) * 4 + x

    def pick(ch, yl, dx):
        col = yl * 512 + dx * 128
        if ch == 0:
            return shared_a[:, col : col + 128]
        if ch < 4:
            whole = (ch - 1) * 1024 + col
            return kvqo[whole // 768][:, whole % 768 : whole % 768 + 128]
        whole = (ch - 4) * 1024 + col
        return w_up[:, whole : whole + 128]

    for yl in range(2):
        for dx in range(4):
            for ch in range(7):
                packed[yl * 4 + dx, :, ch * 128 : ch * 128 + 128] = pick(ch, yl, dx)
    landed[pl.ds(mine, 1)] = packed[pl.ds(mine, 1)]
    pl.semaphore_wait(pltpu.get_barrier_semaphore(), PEERS)
    sends, arrivals = [], []
    for step in range(1, 8):
        dx, dy = step % 4, step // 4
        to = {**at, "x": (x + dx) % 4, "y": (y // 2) * 2 + (y + dy) % 2}
        fro = {**at, "x": (x - dx + 4) % 4, "y": (y // 2) * 2 + (y + dy) % 2}
        to_i, fro_i = (to["y"] % 2) * 4 + to["x"], (fro["y"] % 2) * 4 + fro["x"]
        sends.append(pltpu.make_async_remote_copy(
            src_ref=packed.at[to_i], dst_ref=landed.at[mine], send_sem=send.at[step], recv_sem=recv.at[step],
            device_id=device(to), device_id_type=MESH))
        arrivals.append(pltpu.make_async_remote_copy(
            src_ref=packed.at[to_i], dst_ref=landed.at[fro_i], send_sem=send.at[step], recv_sem=recv.at[step],
            device_id=device(to), device_id_type=MESH))
    other = {**at, "x": x + 1 - 2 * (x % 2)}
    col = pl.ds(pl.multiple_of((1 - x % 2) * 384, 128), 384)
    for k, (src, dst) in enumerate(((w_down.at[:, col], half_d), (shared_b.at[:, col], half_b))):
        sends.append(pltpu.make_async_remote_copy(
            src_ref=src, dst_ref=dst, send_sem=send.at[8 + k], recv_sem=recv.at[8 + k],
            device_id=device(other), device_id_type=MESH))
        arrivals.append(sends[-1])
    for copy in sends:
        copy.start()
    for copy in arrivals:
        copy.wait_recv()
    for i in range(8):
        rows[6 * i : 6 * i + 6, :] = landed[i].astype(F32)
    yh, yl = y // 2, y % 2
    block = rows[...].astype(BF).reshape(3, 16, 896)
    own = pl.ds(pl.multiple_of(x * 128, 128), 128)
    for ch in range(7):
        bufs["panel"][ch, yl, yh, c, z, :, :, own] = block[:, :, ch * 128 : ch * 128 + 128]
    keep = pl.ds(pl.multiple_of((x % 2) * 384, 128), 384)
    even = x % 2 == 0
    for src, got, kind in ((w_down, half_d, "down"), (shared_b, half_b, "up_b")):
        a, b = src[:, keep].astype(F32), got[...].astype(F32)
        pair = jnp.concatenate([jnp.where(even, a, b), jnp.where(even, b, a)], axis=0).astype(BF)
        if kind == "down":
            bufs[kind][yh, c, z, yl, x // 2, :, :, keep] = pair.reshape(3, 16, 384)
        else:
            bufs[kind][yh, c, z, yl, x // 2, :, keep] = pair
    for copy in sends:
        copy.wait_send()


PANEL = (7, 2, 2, 2, 4, 3, 16, 512)
DOWN = (2, 2, 4, 2, 2, 3, 16, 768)
UP_B = (2, 2, 4, 2, 2, 16, 768)


LOG2E = 1.4426950408889634
SCALE_Q = 0.125 * LOG2E
NT = (((1,), (1,)), ((), ()))
TN = (((0,), (0,)), ((), ()))
NN = (((1,), (0,)), ((), ()))
FAR = -1e30


def dot(left, right, dims=NN):
    return lax.dot_general(left, right, dims, preferred_element_type=F32)


def span(start, size):
    return pl.ds(pl.multiple_of(start, size), size)


def panel_of(s, ch, half, cols=slice(None)):
    part = s["panel"][ch, half, :, :, :, :, :, cols]
    return part.reshape(768, part.shape[-1])


def first_half(width=128):
    return lax.broadcasted_iota(jnp.int32, (1, width), 1) < 64


def rank_down(s):
    def half(i, _):
        hb, m = i // 2, i % 2
        rows, cols = span(m * 512, 512), span(hb * 512, 512)
        lat = dot(s["x"][m], panel_of(s, 0, hb))
        s["lat"][rows, cols] = lat.astype(BF)
        s["e"][2 * m + hb] = (lat * s["scale_dq"][:, cols]).astype(BF)
        s["e"][4 + 2 * m + hb] = (lat * s["scale_dv"][:, cols]).astype(BF)
        return 0

    lax.fori_loop(0, 4, half, 0)


def project_keys(s):
    x = s["x"][...].reshape(1024, 768)
    s["qkv"][:, 0:512] = dot(x, panel_of(s, 1, 0)).astype(BF)
    s["qkv"][:, 512:768] = dot(x, panel_of(s, 1, 1, slice(0, 256))).astype(BF)


def project_vera(s, slot, base, tile, ch, half, off, scale, kept, factor):
    cols = slice(tile * 256, tile * 256 + 256)
    up = s["up_b"][:, :, :, :, :, :, cols].reshape(1024, 256)

    def micro(m, _):
        rows = span(m * 512, 512)
        t = dot(s["e"][slot + 2 * m], up[:512]) + dot(s["e"][slot + 2 * m + 1], up[512:])
        s[kept][rows, cols] = t.astype(BF)
        full = dot(s["x"][m], panel_of(s, ch, half, slice(off, off + 256))) + s[scale][:, cols] * t
        s["qkv"][rows, base + tile * 256 : base + tile * 256 + 256] = (full * factor if factor else full).astype(BF)
        return 0

    lax.fori_loop(0, 2, micro, 0)


def project_values(s):
    for tile, (ch, half, off) in enumerate(((1, 1, 256), (2, 0, 0), (2, 0, 256))):
        project_vera(s, 4, 768, tile, ch, half, off, "scale_bv", "vt", None)


def project_queries(s, tiles):
    for tile, (ch, half, off) in enumerate(((2, 1, 0), (2, 1, 256), (3, 0, 0))):
        if tile in tiles:
            project_vera(s, 0, 1536, tile, ch, half, off, "scale_bq", "qt", SCALE_Q)


def masks(s, m):
    pos = lax.broadcasted_iota(jnp.int32, (512, 128), 0)
    lane = lax.broadcasted_iota(jnp.int32, (512, 128), 1) % 64
    end = jnp.int32(0)
    pair = jnp.zeros((512, 128), jnp.int32)
    for p in range(4):
        end = end + s["parts"][m, 0, 2 * p] + s["parts"][m, 0, 2 * p + 1]
        pair = pair + (pos >= end).astype(jnp.int32)
    own = lane == pair
    s["mq"][...] = jnp.where(own, 1.0, 0.0).astype(BF)
    s["mk"][...] = jnp.where(own | (lane >= 8), 0.0, FAR).astype(BF)


def scores(s, buf, rows, p, h):
    mine = first_half() if h == 0 else ~first_half()
    k = jnp.where(mine, s["qkv"][rows, span(p * 128, 128)], s["mk"][...])
    q = jnp.where(mine, s["qkv"][rows, span(1536 + p * 128, 128)], s["mq"][...])
    buf[:, :512] = dot(q, k, NT)


def mix(s, buf, rows, p, h, slot):
    mine = first_half() if h == 0 else ~first_half()
    v = s["qkv"][rows, span(768 + p * 128, 128)]
    sc = buf[:, :512]
    e = jnp.exp2(sc - jnp.max(sc, axis=1, keepdims=True)).astype(BF)
    s["e"][slot] = e
    return dot(e, jnp.where(mine, v, jnp.ones_like(v)))


def attend(s):
    def micro(m, _):
        masks(s, m)
        rows = span(m * 512, 512)
        scores(s, s["f_a"], rows, 0, 0)

        def pair(p, _):
            cols = span(p * 128, 128)
            scores(s, s["g_one"].at[0:512, :], rows, p, 1)
            o0 = mix(s, s["f_a"], rows, p, 0, m * 12 + 2 * p)
            scores(s, s["f_a"], rows, jnp.minimum(p + 1, 5), 0)
            o1 = mix(s, s["g_one"].at[0:512, :], rows, p, 1, m * 12 + 2 * p + 1)
            total = pltpu.roll(jnp.where(first_half(), o1, o0), 64, 1)
            inverse = 1.0 / total
            s["inv"][rows, cols] = inverse.astype(BF)
            s["att"][rows, cols] = (jnp.where(first_half(), o0, o1) * inverse).astype(BF)
            return 0

        lax.fori_loop(0, 6, pair, 0)
        return 0

    lax.fori_loop(0, 2, micro, 0)


def mean(v):
    return jnp.mean(v, axis=1, keepdims=True)


def norm(v):
    centred = v - mean(v)
    r = lax.rsqrt(mean(centred * centred) + 1e-05)
    return centred * r, r


def norm_back(hat, r, g):
    return r * (g - mean(g) - hat * mean(g * hat))


def by_rows(fn, size=128):
    lax.fori_loop(0, 512 // size, lambda i, _: (fn(span(i * size, size)), 0)[1], 0)


def middle(s, m):
    rows = span(m * 512, 512)
    hat, hid, slope = s["f_a"], s["hid"], s["slope"]
    other, low, inv = s["g_one"].at[rows, :], s["ga"].at[rows, :], s["inv"].at[rows, :]
    x, cot = s["x"].at[m], s["cot"].at[m]
    att = s["att"][rows, :]
    hat[:, 0:256] = dot(att, panel_of(s, 3, 0, slice(256, 512)))
    hat[:, 256:768] = dot(att, panel_of(s, 3, 1))

    def norm_one(r):
        n, r1 = norm(x[r, :].astype(F32) + hat[r, :])
        hat[r, :] = n
        low[r, :] = (n * s["gain_one"][...] + s["shift_one"][...]).astype(BF)
        s["r1"][r, :] = r1

    by_rows(norm_one)

    def up(t, _):
        u = dot(low[...], panel_of(s, 4 + t // 2, t % 2))
        cdf = 0.5 * (1.0 + lax.erf(u * 0.7071067811865476))
        cols = span(t * 512, 512)
        hid[:, cols] = (u * cdf).astype(BF)
        slope[:, cols] = (cdf + u * (jnp.exp(-0.5 * u * u) * 0.3989422804014327)).astype(BF)
        return 0

    lax.fori_loop(0, 6, up, 0)
    other[...] = dot(hid[...], s["down"][...].reshape(3072, 768))

    def norm_two(r):
        n2, r2 = norm(hat[r, :] * s["gain_one"][...] + s["shift_one"][...] + other[r, :])
        x[r, :] = (n2 * s["gain_two"][...] + s["shift_two"][...]).astype(BF)
        g = norm_back(n2, r2, cot[r, :].astype(F32) * s["gain_two"][...])
        other[r, :] = g
        low[r, :] = g.astype(BF)

    by_rows(norm_two)

    def back(t, _):
        w = s["down"][t // 2, t % 2].reshape(768, 768)
        cols = span(t * 768, 768)
        hid[:, cols] = (dot(low[...], w, NT) * slope[:, cols].astype(F32)).astype(BF)
        return 0

    lax.fori_loop(0, 4, back, 0)

    def first(t, _):
        other[...] += dot(hid[:, span(t * 512, 512)], panel_of(s, 4 + t // 2, t % 2), NT)
        return 0

    lax.fori_loop(0, 6, first, 0)

    def norm_one_back(r):
        g = norm_back(hat[r, :], s["r1"][r, :], other[r, :] * s["gain_one"][...])
        other[r, :] = g
        low[r, :] = g.astype(BF)

    by_rows(norm_one_back)
    hat[...] = dot(low[:, :256], panel_of(s, 3, 0, slice(256, 512)), NT) + dot(low[:, 256:], panel_of(s, 3, 1), NT)

    def scale_att(r):
        low[r, :] = (hat[r, :] * inv[r, :].astype(F32)).astype(BF)

    by_rows(scale_att)


def attend_back(s):
    def micro(m, _):
        rows = span(m * 512, 512)

        def pair(p, _):
            kc, vc, qc = span(p * 128, 128), span(768 + p * 128, 128), span(1536 + p * 128, 128)
            k, v, q = s["qkv"][rows, kc], s["qkv"][rows, vc], s["qkv"][rows, qc]
            ga = s["ga"][rows, kc]
            prod = ga.astype(F32) * s["att"][rows, kc].astype(F32)
            gq = gk = gv = None
            lanes = lax.broadcasted_iota(jnp.int32, (1, 128), 1)
            for h in range(2):
                mine = first_half() if h == 0 else ~first_half()
                delta = -jnp.sum(jnp.where(mine, prod, 0.0), axis=1, keepdims=True)
                high = delta.astype(BF)
                rest = (delta - high.astype(F32)).astype(BF)
                zero = jnp.zeros_like(ga)
                gah = jnp.where(mine, ga, zero)
                aug = jnp.where(mine, ga, jnp.where(lanes % 64 == 0, high, jnp.where(lanes % 64 == 1, rest, zero)))
                gp = dot(aug, jnp.where(mine, v, jnp.ones_like(v)), NT)
                e = s["e"][m * 12 + 2 * p + h]
                gs = (e.astype(F32) * gp).astype(BF)
                gvh = dot(e, gah, TN)
                gqh = dot(gs, jnp.where(mine, k, zero))
                gkh = dot(gs, jnp.where(mine, q, zero), TN)
                gq, gk, gv = (gqh, gkh, gvh) if h == 0 else (gq + gqh, gk + gkh, gv + gvh)
            s["qkv"][rows, qc] = (gq * 0.125).astype(BF)
            s["qkv"][rows, kc] = (gk * (1.0 / LOG2E)).astype(BF)
            s["qkv"][rows, vc] = gv.astype(BF)
            return 0

        lax.fori_loop(0, 6, pair, 0)
        return 0

    lax.fori_loop(0, 2, micro, 0)


def vera_back(s):
    for base, kept, scale, row, keep in ((1536, "qt", "scale_bq", 1, "att"), (768, "vt", "scale_bv", 3, "ga")):

        def block(i, total):
            rows = span(i * 128, 128)
            g = s["qkv"][rows, base : base + 768].astype(F32)
            s[keep][rows, :] = (g * s[scale][...]).astype(BF)
            return total + jnp.sum(g * s[kept][rows, :].astype(F32), axis=0, keepdims=True)

        s["red"][row : row + 1, 0:768] = lax.fori_loop(0, 8, block, jnp.zeros((1, 768), F32))

    def half(hb, _):
        cols = span(hb * 512, 512)
        w = s["up_b"][hb].reshape(512, 768)
        for m in range(2):
            rows = slice(m * 512, m * 512 + 512)
            gqu, gvu = dot(s["att"][rows, :], w, NT), dot(s["ga"][rows, :], w, NT)
            lat = s["lat"][rows, cols].astype(F32)
            for row, val in ((0, gqu), (2, gvu)):
                part = jnp.sum(val * lat, axis=0, keepdims=True)
                if m:
                    part = part + s["red"][row : row + 1, cols]
                s["red"][row : row + 1, cols] = part
            s["e"][2 * m + hb] = (gqu * s["scale_dq"][:, cols] + gvu * s["scale_dv"][:, cols]).astype(BF)
        return 0

    lax.fori_loop(0, 2, half, 0)


def token_grads(s, m):
    rows = slice(m * 512, m * 512 + 512)
    total = s["f_a"]

    def projections(i, _):
        total[...] += dot(s["qkv"][rows, span(i * 512, 512)], panel_of(s, 1 + i // 2, i % 2), NT)
        return 0

    def latents(hb, _):
        total[...] += dot(s["e"][2 * m + hb], panel_of(s, 0, hb), NT)
        return 0

    total[...] = s["g_one"][rows, :] + dot(s["qkv"][rows, 2048:2304], panel_of(s, 3, 0, slice(0, 256)), NT)
    lax.fori_loop(0, 4, projections, 0)
    lax.fori_loop(0, 2, latents, 0)
    s["cot"][m] = total[...].astype(BF)


LAYER_SCRATCH = dict(
    panel=(PANEL, BF),
    down=(DOWN, BF),
    up_b=(UP_B, BF),
    x=((2, 512, 768), BF),
    cot=((2, 512, 768), BF),
    lat=((1024, 1024), BF),
    qt=((1024, 768), BF),
    vt=((1024, 768), BF),
    qkv=((1024, 2304), BF),
    e=((24, 512, 512), BF),
    att=((1024, 768), BF),
    inv=((1024, 768), BF),
    ga=((1024, 768), BF),
    g_one=((1024, 768), F32),
    f_a=((512, 768), F32),
    hid=((512, 3072), BF),
    slope=((512, 3072), BF),
    mq=((512, 128), BF),
    mk=((512, 128), BF),
    r1=((512, 1), F32),
    red=((4, 1024), F32),
)


VECTORS = ("gain_one", "shift_one", "gain_two", "shift_two", "scale_dq", "scale_bq", "scale_dv", "scale_bv")
SHARDS = ("w_query", "w_key", "w_value", "w_out", "w_up", "w_down", "shared_a", "shared_b")
SHARD_SHAPES = ((6, 768),) * 4 + ((6, 3072), (24, 768), (6, 1024), (8, 768))
GROUP_A, GROUP_1, GROUP_2, GROUP_3 = (("panel", i, i + 1) for i in range(4))
GROUP_UP, GROUP_DOWN, GROUP_B = ("panel", 4, 7), ("down", 0, 0), ("up_b", 0, 0)
EARLY, LATE = (("panel", 0, 4), GROUP_B), (GROUP_UP, GROUP_DOWN)


def reduce_start(at, axis, first, s, send, recv):
    size = 2 if axis == "c" else 4
    here = at[axis]
    s["sums"][pl.ds(first + here, 1)] = s["red"][...][None]
    sends, arrivals = [], []
    for i, delta in enumerate((1, 3, 2) if size == 4 else (1,)):
        to, fro = moved(at, axis, delta), moved(at, axis, -delta)
        for found, slot in ((sends, here), (arrivals, fro[axis])):
            found.append(pltpu.make_async_remote_copy(
                src_ref=s["sums"].at[first + slot], dst_ref=s["sums"].at[first + slot],
                send_sem=send.at[first + i], recv_sem=recv.at[first + i],
                device_id=device(to), device_id_type=MESH))
    for copy in sends:
        copy.start()
    return sends, arrivals, first, size


def reduce_end(state, s):
    sends, arrivals, first, size = state
    for copy in arrivals:
        copy.wait_recv()
    for copy in sends:
        copy.wait_send()
    total = s["sums"][first] + s["sums"][first + 1]
    if size == 4:
        total = total + (s["sums"][first + 2] + s["sums"][first + 3])
    s["red"][...] = total


EXTRA = dict(
    packed=((8, 6, 896), BF),
    landed=((8, 6, 896), BF),
    half_d=((24, 384), BF),
    half_b=((8, 384), BF),
    rows=((48, 896), F32),
    sums=((14, 4, 1024), F32),
)


def whole(*refs):
    names = ("tokens", "parts_in", "cotangent") + tuple("in_" + n for n in SHARDS) + tuple("in_" + n for n in VECTORS)
    names += ("out", "grad_tokens", "grad_red")
    scratch = tuple(LAYER_SCRATCH) + tuple(EXTRA) + SHARDS + VECTORS
    names += scratch + ("parts", "loads", "send_0", "recv_0", "send", "recv", "send_r", "recv_r")
    s = dict(zip(names, refs, strict=True))
    at = place()
    loads = []
    pairs = [(s["in_" + n], s[n]) for n in SHARDS] + [(s["in_" + n], s[n].at[0]) for n in VECTORS]
    pairs += [(s["parts_in"], s["parts"]), (s["tokens"], s["x"]), (s["cotangent"], s["cot"])]
    for i, (src, dst) in enumerate(pairs):
        loads.append(pltpu.make_async_copy(src, dst, s["loads"].at[i]))
        loads[-1].start()
    enter_signal(at)
    for copy in loads[:8]:
        copy.wait()
    bufs = {k: s[k] for k in ("panel", "down", "up_b")}
    stage_zero(at, [s[n] for n in SHARDS], s["packed"], s["landed"], s["half_d"], s["half_b"], s["rows"], bufs, s["send_0"], s["recv_0"])
    moves = Moves(at, bufs, s["send"], s["recv"])
    begun = []

    def start(group, phase):
        moves.start(group, phase)
        begun.append((group, phase))

    for group in EARLY + LATE:
        start(group, 0)
    for group in EARLY + LATE:
        moves.wait(group, 0)
    for group in EARLY + LATE:
        start(group, 1)
    for group in EARLY:
        moves.wait(group, 1)
    order = (GROUP_A, GROUP_1, GROUP_2, GROUP_B, GROUP_3)
    for group in order:
        start(group, 2)
    for group in LATE:
        moves.wait(group, 1)
    for group in LATE:
        start(group, 2)

    def pass_on(group):
        moves.wait(group, 2)
        start(group, 3)

    pass_on(GROUP_A)
    pass_on(GROUP_1)
    for copy in loads[8:]:
        copy.wait()
    moves.wait(GROUP_A, 3)
    rank_down(s)
    pass_on(GROUP_2)
    moves.wait(GROUP_1, 3)
    project_keys(s)
    pass_on(GROUP_B)
    pass_on(GROUP_3)
    moves.wait(GROUP_2, 3)
    moves.wait(GROUP_B, 3)
    project_values(s)
    project_queries(s, (0, 1))
    moves.wait(GROUP_3, 3)
    project_queries(s, (2,))
    attend(s)
    pass_on(GROUP_UP)
    pass_on(GROUP_DOWN)
    moves.wait(GROUP_UP, 3)
    moves.wait(GROUP_DOWN, 3)
    lax.fori_loop(0, 2, lambda m, _: (middle(s, m), 0)[1], 0)
    result = pltpu.make_async_copy(s["x"], s["out"], s["loads"].at[0])
    result.start()
    for group, phase in begun:
        moves.sent(group, phase)
    attend_back(s)
    vera_back(s)
    for row in (1, 3):
        s["red"][row : row + 1, 768:1024] = jnp.zeros((1, 256), F32)
    state = reduce_start(at, "c", 0, s, s["send_r"], s["recv_r"])
    token_grads(s, 0)
    reduce_end(state, s)
    state = reduce_start(at, "x", 2, s, s["send_r"], s["recv_r"])
    token_grads(s, 1)
    grads = pltpu.make_async_copy(s["cot"], s["grad_tokens"], s["loads"].at[1])
    grads.start()
    reduce_end(state, s)
    for axis, first in (("y", 6), ("z", 10)):
        reduce_end(reduce_start(at, axis, first, s, s["send_r"], s["recv_r"]), s)
    last = pltpu.make_async_copy(s["red"], s["grad_red"], s["loads"].at[2])
    last.start()
    assert len(moves.slots) == 124
    for copy in (last, result, grads):
        copy.wait()


def shards(tokens, parts, cotangent, *rest):
    anywhere = pl.BlockSpec(memory_space=pl.ANY)
    scratch = [pltpu.VMEM(shape, kind) for shape, kind in (*LAYER_SCRATCH.values(), *EXTRA.values())]
    scratch += [pltpu.VMEM(shape, BF) for shape in SHARD_SHAPES]
    scratch += [pltpu.VMEM((1, v.shape[0]), F32) for v in rest[8:]]
    scratch += [pltpu.SMEM((2, 1, 8), jnp.int32)]
    scratch += [pltpu.SemaphoreType.DMA((n,)) for n in (19, 10, 10, 124, 124, 14, 14)]
    out, grad, red = pl.pallas_call(
        whole,
        out_shape=[
            jax.ShapeDtypeStruct((2, 512, 768), BF),
            jax.ShapeDtypeStruct((2, 512, 768), BF),
            jax.ShapeDtypeStruct((4, 1024), F32),
        ],
        in_specs=[anywhere] * 19,
        out_specs=[anywhere] * 3,
        scratch_shapes=scratch,
        compiler_params=pltpu.CompilerParams(collective_id=0, has_side_effects=True, vmem_limit_bytes=63 << 20),
    )(tokens, parts, cotangent, *rest)
    return out, grad, red[0], red[1, :768], red[2], red[3, :768]


def solution(mesh):
    rows, split, same = P(None, ("dp", "fsdp"), None), P(("dp", "fsdp"), None), P()
    return jax.shard_map(
        shards,
        mesh=mesh,
        in_specs=(rows,) * 3 + (split,) * 8 + (same,) * 8,
        out_specs=(rows, rows, same, same, same, same),
        check_vma=False,
    )
```

```python
import jax
import jax.numpy as jnp
from jax import lax
from jax.experimental import pallas as pl
from jax.experimental.pallas import tpu as pltpu
from jax.sharding import PartitionSpec as P

MESH = pl.DeviceIdType.MESH
BF = jnp.bfloat16
F32 = jnp.float32


def place():
    dp = lax.axis_index("dp")
    fs = lax.axis_index("fsdp")
    return dict(x=fs % 4, y=(dp // 2) * 2 + (fs // 4) % 2, z=fs // 8, c=dp % 2)


def device(at):
    return ((at["y"] // 2) * 2 + at["c"], at["z"] * 8 + (at["y"] % 2) * 4 + at["x"])


def moved(at, axis, delta):
    size = 2 if axis == "c" else 4
    return {**at, axis: (at[axis] + delta + size) % size}


ORDERS = (("x", "y", "z"), ("y", "z", "x"), ("z", "x", "y"))
PEERS = 23


def near(at):
    for step in range(1, 8):
        x, yl = (at["x"] + step) % 4, (at["y"] + step // 4) % 2
        yield {**at, "x": x, "y": (at["y"] // 2) * 2 + yl}


def across(at):
    for step in range(1, 16):
        yh, c = (at["y"] // 2 + step // 8) % 2, (at["c"] + step // 4) % 2
        yield {**at, "y": yh * 2 + at["y"] % 2, "c": c, "z": (at["z"] + step) % 4}


def peers(at):
    return [*near(at), *across(at), {**at, "y": 3 - at["y"]}]


def enter_signal(at):
    for peer in peers(at):
        pl.semaphore_signal(pltpu.get_barrier_semaphore(), inc=1, device_id=device(peer), device_id_type=MESH)


def region(buf, kind, rot, done, at, low, high):
    every = slice(None)
    x, y, z, c = at["x"], at["y"], at["z"], at["c"]
    yh = every if "y" in done else y // 2
    yl = every if "y" in done else y % 2
    zs = every if "z" in done else z
    if kind == "panel":
        col = every if "x" in done else pl.ds(pl.multiple_of(x * 128, 128), 128)
        return buf.at[low:high, yl, yh, c, zs, rot, :, col]
    half = every if "x" in done else x // 2
    if kind == "down":
        col = every if "x" in done else pl.ds(pl.multiple_of((x % 2) * 384, 128), 384)
        return buf.at[yh, c, zs, yl, half, rot, :, col]
    col = every if "x" in done else pl.ds(pl.multiple_of((x % 2) * 128, 128), 128)
    return buf.at[rot, yh, c, zs, yl, half, :, col]


class Moves:
    def __init__(self, at, bufs, send, recv):
        self.at, self.bufs, self.send, self.recv = at, bufs, send, recv
        self.slots = {}

    def slot(self, key):
        return self.slots.setdefault(key, len(self.slots))

    def copies(self, group, phase):
        kind, low, high = group
        buf = self.bufs[kind]
        for rot in range(3):
            order = ORDERS[rot]
            axis, done = order[phase], order[:phase]
            for delta in (1, 3, 2):
                k = self.slot((group, phase, rot, delta))
                yield (
                    region(buf, kind, rot, done, self.at, low, high),
                    moved(self.at, axis, delta),
                    region(buf, kind, rot, done, moved(self.at, axis, -delta), low, high),
                    k,
                )

    def sibling(self, group):
        kind, low, high = group
        buf = self.bufs[kind]
        k = self.slot((group, "c"))
        for here in (self.at,):
            other = moved(here, "c", 1)
            if kind == "panel":
                mine, theirs = buf.at[low:high, :, :, here["c"]], buf.at[low:high, :, :, other["c"]]
            elif kind == "up_b":
                mine, theirs = buf.at[:, :, here["c"]], buf.at[:, :, other["c"]]
            else:
                mine, theirs = buf.at[:, here["c"]], buf.at[:, other["c"]]
            yield mine, other, theirs, k

    def make(self, what):
        mine, target, theirs, k = what
        return pltpu.make_async_remote_copy(
            src_ref=mine,
            dst_ref=mine,
            send_sem=self.send.at[k],
            recv_sem=self.recv.at[k],
            device_id=device(target),
            device_id_type=MESH,
        )

    def arrival(self, what):
        mine, target, theirs, k = what
        return pltpu.make_async_remote_copy(
            src_ref=theirs,
            dst_ref=theirs,
            send_sem=self.send.at[k],
            recv_sem=self.recv.at[k],
            device_id=device(target),
            device_id_type=MESH,
        )

    def listed(self, group, phase):
        return self.sibling(group) if phase == 3 else self.copies(group, phase)

    def start(self, group, phase):
        for what in self.listed(group, phase):
            self.make(what).start()

    def wait(self, group, phase):
        for what in self.listed(group, phase):
            self.arrival(what).wait_recv()

    def sent(self, group, phase):
        for what in self.listed(group, phase):
            self.make(what).wait_send()


def stage_zero(at, shards, packed, landed, half_d, half_b, both_b, rows, bufs, send, recv):
    w_query, w_key, w_value, w_out, w_up, w_down, shared_a, shared_b = shards
    kvqo = (w_key, w_value, w_query, w_out)
    x, y, z, c = at["x"], at["y"], at["z"], at["c"]
    mine = (y % 2) * 4 + x

    def pick(ch, yl, dx):
        col = yl * 512 + dx * 128
        if ch == 0:
            return shared_a[:, col : col + 128]
        if ch < 4:
            start = (ch - 1) * 256 + col % 256
            return kvqo[col // 256][:, start : start + 128]
        start = (ch - 4) * 1024 + col
        return w_up[:, start : start + 128]

    for yl in range(2):
        for dx in range(4):
            for ch in range(7):
                packed[yl * 4 + dx, :, ch * 128 : ch * 128 + 128] = pick(ch, yl, dx)
    for odd in range(2):
        for r in range(3):
            both_b[odd, :, r * 128 : r * 128 + 128] = shared_b[:, r * 256 + odd * 128 : r * 256 + odd * 128 + 128]
    landed[pl.ds(mine, 1)] = packed[pl.ds(mine, 1)]
    pl.semaphore_wait(pltpu.get_barrier_semaphore(), PEERS)
    sends, arrivals = [], []
    for step in range(1, 8):
        dx, dy = step % 4, step // 4
        to = {**at, "x": (x + dx) % 4, "y": (y // 2) * 2 + (y + dy) % 2}
        fro = {**at, "x": (x - dx + 4) % 4, "y": (y // 2) * 2 + (y + dy) % 2}
        to_i, fro_i = (to["y"] % 2) * 4 + to["x"], (fro["y"] % 2) * 4 + fro["x"]
        sends.append(pltpu.make_async_remote_copy(
            src_ref=packed.at[to_i], dst_ref=landed.at[mine], send_sem=send.at[step], recv_sem=recv.at[step],
            device_id=device(to), device_id_type=MESH))
        arrivals.append(pltpu.make_async_remote_copy(
            src_ref=packed.at[to_i], dst_ref=landed.at[fro_i], send_sem=send.at[step], recv_sem=recv.at[step],
            device_id=device(to), device_id_type=MESH))
    other = {**at, "x": x + 1 - 2 * (x % 2)}
    col = pl.ds(pl.multiple_of((1 - x % 2) * 384, 128), 384)
    for k, (src, dst) in enumerate(((w_down.at[:, col], half_d), (both_b.at[1 - x % 2], half_b))):
        sends.append(pltpu.make_async_remote_copy(
            src_ref=src, dst_ref=dst, send_sem=send.at[8 + k], recv_sem=recv.at[8 + k],
            device_id=device(other), device_id_type=MESH))
        arrivals.append(sends[-1])
    for copy in sends:
        copy.start()
    for copy in arrivals:
        copy.wait_recv()
    for i in range(8):
        rows[6 * i : 6 * i + 6, :] = landed[i].astype(F32)
    yh, yl = y // 2, y % 2
    block = rows[...].astype(BF).reshape(3, 16, 896)
    own = pl.ds(pl.multiple_of(x * 128, 128), 128)
    for ch in range(7):
        bufs["panel"][ch, yl, yh, c, z, :, :, own] = block[:, :, ch * 128 : ch * 128 + 128]
    keep = pl.ds(pl.multiple_of((x % 2) * 384, 128), 384)
    lane = pl.ds(pl.multiple_of((x % 2) * 128, 128), 128)

    def joined(mine_too, got):
        a, b = mine_too.astype(F32), got[...].astype(F32)
        even = x % 2 == 0
        return jnp.concatenate([jnp.where(even, a, b), jnp.where(even, b, a)], axis=0).astype(BF)

    bufs["down"][yh, c, z, yl, x // 2, :, :, keep] = joined(w_down[:, keep], half_d).reshape(3, 16, 384)
    pair = joined(both_b[x % 2], half_b)
    for r in range(3):
        bufs["up_b"][r, yh, c, z, yl, x // 2, :, lane] = pair[:, r * 128 : r * 128 + 128]
    for copy in sends:
        copy.wait_send()


PANEL = (7, 2, 2, 2, 4, 3, 16, 512)
DOWN = (2, 2, 4, 2, 2, 3, 16, 768)
UP_B = (3, 2, 2, 4, 2, 2, 16, 256)


LOG2E = 1.4426950408889634
SCALE_Q = 0.125 * LOG2E
NT = (((1,), (1,)), ((), ()))
TN = (((0,), (0,)), ((), ()))
NN = (((1,), (0,)), ((), ()))
FAR = -1e30
GRADS = ("hid", "slope")


def dot(left, right, dims=NN):
    return lax.dot_general(left, right, dims, preferred_element_type=F32)


def span(start, size):
    return pl.ds(pl.multiple_of(start, size), size)


def panel_of(s, ch, half, cols=slice(None)):
    part = s["panel"][ch, half, :, :, :, :, :, cols]
    return part.reshape(768, part.shape[-1])


def first_half(width=128):
    return lax.broadcasted_iota(jnp.int32, (1, width), 1) < 64


def rank_down(s):
    def half(hb, _):
        cols = span(hb * 512, 512)
        lat = dot(s["x"][...].reshape(1024, 768), panel_of(s, 0, hb))
        s["lat"][:, cols] = lat.astype(BF)
        for slot, name in ((8, "scale_dq"), (20, "scale_dv")):
            s["e"][pl.ds(slot + 2 * hb, 2)] = (lat * s[name][:, cols]).astype(BF).reshape(2, 512, 512)
        return 0

    lax.fori_loop(0, 2, half, 0)


def project(s, r):
    cols, base = slice(r * 256, r * 256 + 256), r * 768
    x = s["x"][...].reshape(1024, 768)
    s["qkv"][:, base : base + 256] = dot(x, panel_of(s, 1 + r, 0, slice(0, 256))).astype(BF)
    for slot, half, off, scale, kept, at, factor in (
        (20, 0, 256, "scale_bv", "vt", 256, None),
        (8, 1, 0, "scale_bq", "qt", 512, SCALE_Q),
    ):
        low, high = (s["e"][slot + 2 * hb : slot + 2 * hb + 2].reshape(1024, 512) for hb in range(2))
        up = s["up_b"][r].reshape(1024, 256)
        t = dot(low, up[:512]) + dot(high, up[512:])
        s[kept][:, cols] = t.astype(BF)
        full = dot(x, panel_of(s, 1 + r, half, slice(off, off + 256))) + s[scale][:, cols] * t
        s["qkv"][:, base + at : base + at + 256] = (full * factor if factor else full).astype(BF)


def masks(s):
    def micro(m, _):
        pos = lax.broadcasted_iota(jnp.int32, (512, 128), 0)
        lane = lax.broadcasted_iota(jnp.int32, (512, 128), 1) % 64
        end = jnp.int32(0)
        pair = jnp.zeros((512, 128), jnp.int32)
        for p in range(4):
            end = end + s["parts"][m, 0, 2 * p] + s["parts"][m, 0, 2 * p + 1]
            pair = pair + (pos >= end).astype(jnp.int32)
        own = lane == pair
        s["mq"][m] = jnp.where(own, 1.0, 0.0).astype(BF)
        s["mk"][m] = jnp.where(own | (lane >= 8), 0.0, FAR).astype(BF)
        return 0

    lax.fori_loop(0, 2, micro, 0)


def places(r, i):
    m, half = i // 2, i % 2
    base = r * 768 + half * 128
    kvq = [span(base + j * 256, 128) for j in range(3)]
    return m, 2 * r + half, span(m * 512, 512), kvq, span(r * 256 + half * 128, 128)


def scores(s, buf, r, i, h):
    m, _, rows, (kc, _, qc), _ = places(r, i)
    mine = first_half() if h == 0 else ~first_half()
    k = jnp.where(mine, s["qkv"][rows, kc], s["mk"][m])
    q = jnp.where(mine, s["qkv"][rows, qc], s["mq"][m])
    buf[:, :512] = dot(q, k, NT)


def mix(s, buf, r, i, h):
    m, p, rows, (_, vc, _), _ = places(r, i)
    mine = first_half() if h == 0 else ~first_half()
    v = s["qkv"][rows, vc]
    sc = buf[:, :512]
    e = jnp.exp2(sc - jnp.max(sc, axis=1, keepdims=True)).astype(BF)
    s["e"][m * 12 + 2 * p + h] = e
    return dot(e, jnp.where(mine, v, jnp.ones_like(v)))


def attend(s, r):
    s_a, s_b = s["f_a"], s["g_one"].at[0:512, :]
    scores(s, s_a, r, 0, 0)

    def pair(i, _):
        _, _, rows, _, cols = places(r, i)
        scores(s, s_b, r, i, 1)
        o0 = mix(s, s_a, r, i, 0)
        scores(s, s_a, r, jnp.minimum(i + 1, 3), 0)
        o1 = mix(s, s_b, r, i, 1)
        total = pltpu.roll(jnp.where(first_half(), o1, o0), 64, 1)
        inverse = 1.0 / total
        s["inv"][rows, cols] = inverse.astype(BF)
        s["att"][rows, cols] = (jnp.where(first_half(), o0, o1) * inverse).astype(BF)
        return 0

    lax.fori_loop(0, 4, pair, 0, unroll=4)


def mean(v):
    return jnp.mean(v, axis=1, keepdims=True)


def norm(v):
    centred = v - mean(v)
    r = lax.rsqrt(mean(centred * centred) + 1e-05)
    return centred * r, r


def norm_back(hat, r, g):
    return r * (g - mean(g) - hat * mean(g * hat))


def by_rows(fn, size=128):
    for start in range(0, 512, size):
        fn(slice(start, start + size))


def middle(s, m):
    rows = span(m * 512, 512)
    hat, hid, slope = s["f_a"], s["hid"], s["slope"]
    other, low, inv = s["g_one"].at[rows, :], s["ga"].at[rows, :], s["inv"].at[rows, :]
    x, cot = s["x"].at[m], s["cot"].at[m]
    att = s["att"][rows, :]
    for r in range(3):
        hat[:, r * 256 : r * 256 + 256] = dot(att, panel_of(s, 1 + r, 1, slice(256, 512)))

    def norm_one(r):
        n, r1 = norm(x[r, :].astype(F32) + hat[r, :])
        hat[r, :] = n
        low[r, :] = (n * s["gain_one"][...] + s["shift_one"][...]).astype(BF)
        s["r1"][r, :] = r1

    by_rows(norm_one)

    def up(t, _):
        u = dot(low[...], panel_of(s, 4 + t // 2, t % 2))
        cdf = 0.5 + 0.5 * lax.erf(u * 0.7071067811865476)
        cols = span(t * 512, 512)
        hid[:, cols] = (u * cdf).astype(BF)
        slope[:, cols] = (cdf + (u * 0.3989422804014327) * jnp.exp2(u * (u * (-0.5 * LOG2E)))).astype(BF)
        return 0

    lax.fori_loop(0, 6, up, 0, unroll=6)
    other[...] = dot(hid[...], s["down"][...].reshape(3072, 768))

    def norm_two(r):
        n2, r2 = norm(hat[r, :] * s["gain_one"][...] + s["shift_one"][...] + other[r, :])
        x[r, :] = (n2 * s["gain_two"][...] + s["shift_two"][...]).astype(BF)
        g = norm_back(n2, r2, cot[r, :].astype(F32) * s["gain_two"][...])
        other[r, :] = g
        low[r, :] = g.astype(BF)

    by_rows(norm_two)

    def back(t, _):
        w = s["down"][t // 2, t % 2].reshape(768, 768)
        cols = span(t * 768, 768)
        hid[:, cols] = (dot(low[...], w, NT) * slope[:, cols].astype(F32)).astype(BF)
        return 0

    lax.fori_loop(0, 4, back, 0, unroll=4)

    other[...] += sum(dot(hid[:, t * 512 : t * 512 + 512], panel_of(s, 4 + t // 2, t % 2), NT) for t in range(6))

    def norm_one_back(r):
        g = norm_back(hat[r, :], s["r1"][r, :], other[r, :] * s["gain_one"][...])
        other[r, :] = g
        low[r, :] = g.astype(BF)

    by_rows(norm_one_back)
    hat[...] = sum(dot(low[:, r * 256 : r * 256 + 256], panel_of(s, 1 + r, 1, slice(256, 512)), NT) for r in range(3))

    def scale_att(r):
        low[r, :] = (hat[r, :] * inv[r, :].astype(F32)).astype(BF)

    by_rows(scale_att)


def attend_back(s):
    def third(r, _):
        for i in range(4):
            m, p, rows, (kc, vc, qc), cols = places(r, i)
            k, v, q = s["qkv"][rows, kc], s["qkv"][rows, vc], s["qkv"][rows, qc]
            ga = s["ga"][rows, cols]
            prod = ga.astype(F32) * s["att"][rows, cols].astype(F32)
            gq = gk = gv = None
            lanes = lax.broadcasted_iota(jnp.int32, (1, 128), 1)
            for h in range(2):
                mine = first_half() if h == 0 else ~first_half()
                delta = -jnp.sum(jnp.where(mine, prod, 0.0), axis=1, keepdims=True)
                high = delta.astype(BF)
                rest = (delta - high.astype(F32)).astype(BF)
                zero = jnp.zeros_like(ga)
                gah = jnp.where(mine, ga, zero)
                aug = jnp.where(mine, ga, jnp.where(lanes % 64 == 0, high, jnp.where(lanes % 64 == 1, rest, zero)))
                gp = dot(aug, jnp.where(mine, v, jnp.ones_like(v)), NT)
                e = s["e"][m * 12 + 2 * p + h]
                gs = (e.astype(F32) * gp).astype(BF)
                gvh = dot(e, gah, TN)
                gqh = dot(gs, jnp.where(mine, k, zero))
                gkh = dot(gs, jnp.where(mine, q, zero), TN)
                gq, gk, gv = (gqh, gkh, gvh) if h == 0 else (gq + gqh, gk + gkh, gv + gvh)
            to = s[GRADS[m]]
            to[:, qc] = (gq * 0.125).astype(BF)
            to[:, kc] = (gk * (1.0 / LOG2E)).astype(BF)
            to[:, vc] = gv.astype(BF)
        return 0

    lax.fori_loop(0, 3, third, 0)


def vera_back(s):
    for base, kept, scale, row, keep in ((512, "qt", "scale_bq", 1, "att"), (256, "vt", "scale_bv", 3, "ga")):
        for r in range(3):
            cols = slice(r * 256, r * 256 + 256)

            total = jnp.zeros((1, 256), F32)
            for m in range(2):
                rows = slice(m * 512, m * 512 + 512)
                g = s[GRADS[m]][:, r * 768 + base : r * 768 + base + 256].astype(F32)
                s[keep][rows, cols] = (g * s[scale][:, cols]).astype(BF)
                total = total + jnp.sum(g * s[kept][rows, cols].astype(F32), axis=0, keepdims=True)
            s["red"][row : row + 1, cols] = total

    def half(hb, _):
        cols = span(hb * 512, 512)
        for m in range(2):
            rows = slice(m * 512, m * 512 + 512)
            gqu, gvu = (
                sum(dot(s[name][rows, r * 256 : r * 256 + 256], s["up_b"][r, hb].reshape(512, 256), NT) for r in range(3))
                for name in ("att", "ga")
            )
            lat = s["lat"][rows, cols].astype(F32)
            for row, val in ((0, gqu), (2, gvu)):
                part = jnp.sum(val * lat, axis=0, keepdims=True)
                if m:
                    part = part + s["red"][row : row + 1, cols]
                s["red"][row : row + 1, cols] = part
            s["e"][2 * hb + m] = (gqu * s["scale_dq"][:, cols] + gvu * s["scale_dv"][:, cols]).astype(BF)
        return 0

    lax.fori_loop(0, 2, half, 0)


def token_grads(s, m):
    rows = slice(m * 512, m * 512 + 512)
    terms = []
    for r in range(3):
        for j, (half, off) in enumerate(((0, 0), (0, 256), (1, 0))):
            lo = r * 768 + j * 256
            terms.append(dot(s[GRADS[m]][:, lo : lo + 256], panel_of(s, 1 + r, half, slice(off, off + 256)), NT))
    for hb in range(2):
        terms.append(dot(s["e"][2 * hb + m], panel_of(s, 0, hb), NT))
    s["cot"][m] = (s["g_one"][rows, :] + sum(terms)).astype(BF)


LAYER_SCRATCH = dict(
    panel=(PANEL, BF),
    down=(DOWN, BF),
    up_b=(UP_B, BF),
    x=((2, 512, 768), BF),
    cot=((2, 512, 768), BF),
    lat=((1024, 1024), BF),
    qt=((1024, 768), BF),
    vt=((1024, 768), BF),
    qkv=((1024, 2304), BF),
    e=((24, 512, 512), BF),
    att=((1024, 768), BF),
    inv=((1024, 768), BF),
    ga=((1024, 768), BF),
    g_one=((1024, 768), F32),
    f_a=((512, 768), F32),
    hid=((512, 3072), BF),
    slope=((512, 3072), BF),
    mq=((2, 512, 128), BF),
    mk=((2, 512, 128), BF),
    r1=((512, 1), F32),
    red=((4, 1024), F32),
)


VECTORS = ("gain_one", "shift_one", "gain_two", "shift_two", "scale_dq", "scale_bq", "scale_dv", "scale_bv")
SHARDS = ("w_query", "w_key", "w_value", "w_out", "w_up", "w_down", "shared_a", "shared_b")
SHARD_SHAPES = ((6, 768),) * 4 + ((6, 3072), (24, 768), (6, 1024), (8, 768))
GROUP_A, GROUP_1, GROUP_2, GROUP_3 = (("panel", i, i + 1) for i in range(4))
GROUP_UP, GROUP_DOWN, GROUP_B = ("panel", 4, 7), ("down", 0, 0), ("up_b", 0, 0)
FRONT, LATE = ("panel", 0, 4), (GROUP_UP, GROUP_DOWN)


def near_place(at):
    return (at["y"] % 2) * 4 + at["x"]


def across_place(at):
    return 8 + ((at["y"] // 2) * 2 + at["c"]) * 4 + at["z"]


def reduce_start(at, group, place_of, s, send, recv):
    here = place_of(at)
    s["sums"][pl.ds(here, 1)] = s["red"][...][None]
    sends, arrivals = [], []
    for i, other in enumerate(group(at)):
        k = i if place_of is near_place else 7 + i
        for found, slot in ((sends, here), (arrivals, place_of(other))):
            found.append(pltpu.make_async_remote_copy(
                src_ref=s["sums"].at[here], dst_ref=s["sums"].at[slot],
                send_sem=send.at[k], recv_sem=recv.at[place_of(other)] if found is arrivals else recv.at[here],
                device_id=device(other), device_id_type=MESH))
    for copy in sends:
        copy.start()
    return sends, arrivals


def reduce_end(state, first, size, s):
    sends, arrivals = state
    for copy in arrivals:
        copy.wait_recv()
    for copy in sends:
        copy.wait_send()
    values = [s["sums"][first + i] for i in range(size)]
    while len(values) > 1:
        values = [values[i] + values[i + 1] for i in range(0, len(values), 2)]
    s["red"][...] = values[0]


EXTRA = dict(
    packed=((8, 6, 896), BF),
    landed=((8, 6, 896), BF),
    half_d=((24, 384), BF),
    half_b=((8, 384), BF),
    both_b=((2, 8, 384), BF),
    rows=((48, 896), F32),
    sums=((24, 4, 1024), F32),
)


def whole(*refs):
    names = ("tokens", "parts_in", "cotangent") + tuple("in_" + n for n in SHARDS) + tuple("in_" + n for n in VECTORS)
    names += ("out", "grad_tokens", "grad_dq", "grad_bq", "grad_dv", "grad_bv")
    scratch = tuple(LAYER_SCRATCH) + tuple(EXTRA) + SHARDS + VECTORS
    names += scratch + ("parts", "loads", "send_0", "recv_0", "send", "recv", "send_r", "recv_r")
    s = dict(zip(names, refs, strict=True))
    at = place()
    enter_signal(at)
    loads = []
    pairs = [(s["in_" + n], s[n]) for n in SHARDS] + [(s["in_" + n], s[n].at[0]) for n in VECTORS]
    pairs += [(s["parts_in"], s["parts"]), (s["tokens"], s["x"]), (s["cotangent"], s["cot"])]
    for i, (src, dst) in enumerate(pairs):
        loads.append(pltpu.make_async_copy(src, dst, s["loads"].at[i]))
        loads[-1].start()
    for copy in loads[:8]:
        copy.wait()
    bufs = {k: s[k] for k in ("panel", "down", "up_b")}
    stage_zero(at, [s[n] for n in SHARDS], s["packed"], s["landed"], s["half_d"], s["half_b"], s["both_b"], s["rows"], bufs, s["send_0"], s["recv_0"])
    moves = Moves(at, bufs, s["send"], s["recv"])
    begun = []

    def start(group, phase):
        moves.start(group, phase)
        begun.append((group, phase))

    def pass_on(group):
        moves.wait(group, 2)
        start(group, 3)

    start(FRONT, 0)
    start(GROUP_B, 0)
    for group in LATE:
        start(group, 0)
    moves.wait(FRONT, 0)
    start(FRONT, 1)
    moves.wait(GROUP_B, 0)
    start(GROUP_B, 1)
    for group in LATE:
        moves.wait(group, 0)
        start(group, 1)
    moves.wait(FRONT, 1)
    start(GROUP_A, 2)
    start(GROUP_1, 2)
    moves.wait(GROUP_B, 1)
    for group in (GROUP_B, GROUP_2, GROUP_3):
        start(group, 2)
    for copy in loads[8:]:
        copy.wait()
    masks(s)
    pass_on(GROUP_A)
    pass_on(GROUP_1)
    moves.wait(GROUP_A, 3)
    rank_down(s)
    pass_on(GROUP_B)
    moves.wait(GROUP_UP, 1)
    start(GROUP_UP, 2)
    pass_on(GROUP_2)
    moves.wait(GROUP_1, 3)
    moves.wait(GROUP_B, 3)
    project(s, 0)
    pass_on(GROUP_3)
    moves.wait(GROUP_DOWN, 1)
    start(GROUP_DOWN, 2)
    attend(s, 0)
    moves.wait(GROUP_2, 3)
    project(s, 1)
    attend(s, 1)
    moves.wait(GROUP_3, 3)
    project(s, 2)
    pass_on(GROUP_UP)
    attend(s, 2)
    pass_on(GROUP_DOWN)
    moves.wait(GROUP_UP, 3)
    moves.wait(GROUP_DOWN, 3)
    lax.fori_loop(0, 2, lambda m, _: (middle(s, m), 0)[1], 0)
    result = pltpu.make_async_copy(s["x"], s["out"], s["loads"].at[0])
    result.start()
    for group, phase in begun:
        moves.sent(group, phase)
    attend_back(s)
    vera_back(s)
    for row in (1, 3):
        s["red"][row : row + 1, 768:1024] = jnp.zeros((1, 256), F32)
    state = reduce_start(at, near, near_place, s, s["send_r"], s["recv_r"])
    token_grads(s, 0)
    reduce_end(state, 0, 8, s)
    state = reduce_start(at, across, across_place, s, s["send_r"], s["recv_r"])
    token_grads(s, 1)
    ends = [result]
    ends.append(pltpu.make_async_copy(s["cot"], s["grad_tokens"], s["loads"].at[1]))
    ends[-1].start()
    reduce_end(state, 8, 16, s)
    for i, name in enumerate(("grad_dq", "grad_bq", "grad_dv", "grad_bv")):
        ends.append(pltpu.make_async_copy(s["red"].at[i, 0 : s[name].shape[0]], s[name], s["loads"].at[2 + i]))
        ends[-1].start()
    assert len(moves.slots) == 142
    for copy in ends:
        copy.wait()


def hand_over(*refs):
    for src, dst in zip(refs[:6], refs[6:], strict=True):
        dst[...] = src[...]


def shards(tokens, parts, cotangent, *rest):
    anywhere = pl.BlockSpec(memory_space=pl.ANY)
    scratch = [pltpu.VMEM(shape, kind) for shape, kind in (*LAYER_SCRATCH.values(), *EXTRA.values())]
    scratch += [pltpu.VMEM(shape, BF) for shape in SHARD_SHAPES]
    scratch += [pltpu.VMEM((1, v.shape[0]), F32) for v in rest[8:]]
    scratch += [pltpu.SMEM((2, 1, 8), jnp.int32)]
    scratch += [pltpu.SemaphoreType.DMA((n,)) for n in (19, 10, 10, 142, 142, 22, 24)]
    shapes = [jax.ShapeDtypeStruct((2, 512, 768), BF)] * 2
    shapes += [jax.ShapeDtypeStruct((n,), F32) for n in (1024, 768, 1024, 768)]
    found = pl.pallas_call(
        whole,
        out_shape=shapes,
        in_specs=[anywhere] * 19,
        out_specs=[anywhere] * 6,
        scratch_shapes=scratch,
        compiler_params=pltpu.CompilerParams(collective_id=0, has_side_effects=True, vmem_limit_bytes=66900000),
    )(tokens, parts, cotangent, *rest)
    blocks = [pl.BlockSpec((1, 256, 768), lambda i: (i // 2, i % 2, 0))] * 2
    blocks += [pl.BlockSpec((n,), lambda i: (0,)) for n in (1024, 768, 1024, 768)]
    return tuple(pl.pallas_call(hand_over, grid=(4,), out_shape=shapes, in_specs=blocks, out_specs=blocks)(*found))


def solution(mesh):
    rows, split, same = P(None, ("dp", "fsdp"), None), P(("dp", "fsdp"), None), P()
    return jax.shard_map(
        shards,
        mesh=mesh,
        in_specs=(rows,) * 3 + (split,) * 8 + (same,) * 8,
        out_specs=(rows, rows, same, same, same, same),
        check_vma=False,
    )
```

```python
import jax
import jax.numpy as jnp
from jax import lax
from jax.experimental import pallas as pl
from jax.experimental.pallas import tpu as pltpu
from jax.sharding import PartitionSpec as P

MESH = pl.DeviceIdType.MESH
BF = jnp.bfloat16
F32 = jnp.float32


def place():
    dp = lax.axis_index("dp")
    fs = lax.axis_index("fsdp")
    return dict(x=fs % 4, y=(dp // 2) * 2 + (fs // 4) % 2, z=fs // 8, c=dp % 2)


def device(at):
    return ((at["y"] // 2) * 2 + at["c"], at["z"] * 8 + (at["y"] % 2) * 4 + at["x"])


def moved(at, axis, delta):
    size = 2 if axis == "c" else 4
    return {**at, axis: (at[axis] + delta + size) % size}


ORDERS = (("x", "y", "z"), ("y", "z", "x"), ("z", "x", "y"))
PEERS = 23


def near(at):
    for step in range(1, 8):
        x, yl = (at["x"] + step) % 4, (at["y"] + step // 4) % 2
        yield {**at, "x": x, "y": (at["y"] // 2) * 2 + yl}


def across(at):
    for step in range(1, 16):
        yh, c = (at["y"] // 2 + step // 8) % 2, (at["c"] + step // 4) % 2
        yield {**at, "y": yh * 2 + at["y"] % 2, "c": c, "z": (at["z"] + step) % 4}


def peers(at):
    return [*near(at), *across(at), {**at, "y": 3 - at["y"]}]


def enter_signal(at):
    for peer in peers(at):
        pl.semaphore_signal(pltpu.get_barrier_semaphore(), inc=1, device_id=device(peer), device_id_type=MESH)


def region(buf, kind, rot, done, at, low, high):
    every = slice(None)
    x, y, z, c = at["x"], at["y"], at["z"], at["c"]
    yh = every if "y" in done else y // 2
    yl = every if "y" in done else y % 2
    zs = every if "z" in done else z
    col = every if "x" in done else pl.ds(pl.multiple_of(x * 128, 128), 128)
    if kind == "panel":
        return buf.at[low:high, yl, yh, c, zs, rot, :, col]
    col = every if "x" in done else pl.ds(pl.multiple_of((x % 2) * 128, 128), 128)
    xh = every if "x" in done else x // 2
    if kind == "down":
        return buf.at[low:high, yh, c, zs, yl, xh, rot, :, col]
    return buf.at[rot, yh, c, zs, yl, xh, :, col]


class Moves:
    def __init__(self, at, bufs, send, recv):
        self.at, self.bufs, self.send, self.recv = at, bufs, send, recv
        self.slots = {}

    def slot(self, key):
        return self.slots.setdefault(key, len(self.slots))

    def copies(self, group, phase):
        kind, low, high = group
        buf = self.bufs[kind]
        for rot in range(3):
            order = ORDERS[rot]
            axis, done = order[phase], order[:phase]
            for delta in (1, 3, 2):
                k = self.slot((group, phase, rot, delta))
                yield (
                    region(buf, kind, rot, done, self.at, low, high),
                    moved(self.at, axis, delta),
                    region(buf, kind, rot, done, moved(self.at, axis, -delta), low, high),
                    k,
                )

    def sibling(self, group):
        kind, low, high = group
        buf = self.bufs[kind]
        k = self.slot((group, "c"))
        for here in (self.at,):
            other = moved(here, "c", 1)
            if kind == "panel":
                mine, theirs = buf.at[low:high, :, :, here["c"]], buf.at[low:high, :, :, other["c"]]
            elif kind == "up_b":
                mine, theirs = buf.at[:, :, here["c"]], buf.at[:, :, other["c"]]
            else:
                mine, theirs = buf.at[low:high, :, here["c"]], buf.at[low:high, :, other["c"]]
            yield mine, other, theirs, k

    def make(self, what):
        mine, target, theirs, k = what
        return pltpu.make_async_remote_copy(
            src_ref=mine,
            dst_ref=mine,
            send_sem=self.send.at[k],
            recv_sem=self.recv.at[k],
            device_id=device(target),
            device_id_type=MESH,
        )

    def arrival(self, what):
        mine, target, theirs, k = what
        return pltpu.make_async_remote_copy(
            src_ref=theirs,
            dst_ref=theirs,
            send_sem=self.send.at[k],
            recv_sem=self.recv.at[k],
            device_id=device(target),
            device_id_type=MESH,
        )

    def listed(self, group, phase):
        return self.sibling(group) if phase == 3 else self.copies(group, phase)

    def start(self, group, phase):
        for what in self.listed(group, phase):
            self.make(what).start()

    def wait(self, group, phase):
        for what in self.listed(group, phase):
            self.arrival(what).wait_recv()

    def sent(self, group, phase):
        for what in self.listed(group, phase):
            self.make(what).wait_send()


def stage_zero(at, shards, packed, landed, half_d, half_b, both_b, both_d, rows, bufs, send, recv):
    w_query, w_key, w_value, w_out, w_up, w_down, shared_a, shared_b = shards
    kvqo = (w_key, w_value, w_query, w_out)
    x, y, z, c = at["x"], at["y"], at["z"], at["c"]
    mine = (y % 2) * 4 + x

    def pick(ch, yl, dx):
        col = yl * 512 + dx * 128
        if ch == 0:
            return shared_a[:, col : col + 128]
        if ch < 4:
            start = (ch - 1) * 256 + col % 256
            return kvqo[col // 256][:, start : start + 128]
        start = (ch - 4) * 1024 + col
        return w_up[:, start : start + 128]

    for yl in range(2):
        for dx in range(4):
            for ch in range(7):
                packed[yl * 4 + dx, :, ch * 128 : ch * 128 + 128] = pick(ch, yl, dx)
    for odd in range(2):
        for r in range(3):
            tile = slice(r * 256 + odd * 128, r * 256 + odd * 128 + 128)
            both_b[odd, :, r * 128 : r * 128 + 128] = shared_b[:, tile]
            both_d[odd, :, r * 128 : r * 128 + 128] = w_down[:, tile]
    landed[pl.ds(mine, 1)] = packed[pl.ds(mine, 1)]
    pl.semaphore_wait(pltpu.get_barrier_semaphore(), PEERS)
    sends, arrivals = [], []
    for step in range(1, 8):
        dx, dy = step % 4, step // 4
        to = {**at, "x": (x + dx) % 4, "y": (y // 2) * 2 + (y + dy) % 2}
        fro = {**at, "x": (x - dx + 4) % 4, "y": (y // 2) * 2 + (y + dy) % 2}
        to_i, fro_i = (to["y"] % 2) * 4 + to["x"], (fro["y"] % 2) * 4 + fro["x"]
        sends.append(pltpu.make_async_remote_copy(
            src_ref=packed.at[to_i], dst_ref=landed.at[mine], send_sem=send.at[step], recv_sem=recv.at[step],
            device_id=device(to), device_id_type=MESH))
        arrivals.append(pltpu.make_async_remote_copy(
            src_ref=packed.at[to_i], dst_ref=landed.at[fro_i], send_sem=send.at[step], recv_sem=recv.at[step],
            device_id=device(to), device_id_type=MESH))
    other = {**at, "x": x + 1 - 2 * (x % 2)}
    for k, (src, dst) in enumerate(((both_d.at[1 - x % 2], half_d), (both_b.at[1 - x % 2], half_b))):
        sends.append(pltpu.make_async_remote_copy(
            src_ref=src, dst_ref=dst, send_sem=send.at[8 + k], recv_sem=recv.at[8 + k],
            device_id=device(other), device_id_type=MESH))
        arrivals.append(sends[-1])
    for copy in sends:
        copy.start()
    for copy in arrivals:
        copy.wait_recv()
    for i in range(8):
        rows[6 * i : 6 * i + 6, :] = landed[i].astype(F32)
    yh, yl = y // 2, y % 2
    block = rows[...].astype(BF).reshape(3, 16, 896)
    own = pl.ds(pl.multiple_of(x * 128, 128), 128)
    for ch in range(7):
        bufs["panel"][ch, yl, yh, c, z, :, :, own] = block[:, :, ch * 128 : ch * 128 + 128]
    lane = pl.ds(pl.multiple_of((x % 2) * 128, 128), 128)

    def joined(mine_too, got):
        a, b = mine_too.astype(F32), got[...].astype(F32)
        even = x % 2 == 0
        return jnp.concatenate([jnp.where(even, a, b), jnp.where(even, b, a)], axis=0).astype(BF)

    block = joined(both_d[x % 2], half_d).reshape(3, 16, 384)
    for k in range(3):
        bufs["down"][k, yh, c, z, yl, x // 2, :, :, lane] = block[:, :, k * 128 : k * 128 + 128]
    pair = joined(both_b[x % 2], half_b)
    for r in range(3):
        bufs["up_b"][r, yh, c, z, yl, x // 2, :, lane] = pair[:, r * 128 : r * 128 + 128]
    for copy in sends:
        copy.wait_send()


PANEL = (7, 2, 2, 2, 4, 3, 16, 512)
DOWN = (3, 2, 2, 4, 2, 2, 3, 16, 256)
UP_B = (3, 2, 2, 4, 2, 2, 16, 256)


LOG2E = 1.4426950408889634
SCALE_Q = 0.125 * LOG2E
NT = (((1,), (1,)), ((), ()))
TN = (((0,), (0,)), ((), ()))
NN = (((1,), (0,)), ((), ()))
FAR = -1e30
GRADS = ("hid", "slope")


def dot(left, right, dims=NN):
    return lax.dot_general(left, right, dims, preferred_element_type=F32)


def span(start, size):
    return pl.ds(pl.multiple_of(start, size), size)


def panel_of(s, ch, half, cols=slice(None)):
    part = s["panel"][ch, half, :, :, :, :, :, cols]
    return part.reshape(768, part.shape[-1])


def first_half(width=128):
    return lax.broadcasted_iota(jnp.int32, (1, width), 1) < 64


def rank_down(s):
    def half(hb, _):
        cols = span(hb * 512, 512)
        lat = dot(s["x"][...].reshape(1024, 768), panel_of(s, 0, hb))
        s["lat"][:, cols] = lat.astype(BF)
        for slot, name in ((8, "scale_dq"), (20, "scale_dv")):
            s["e"][pl.ds(slot + 2 * hb, 2)] = (lat * s[name][:, cols]).astype(BF).reshape(2, 512, 512)
        return 0

    lax.fori_loop(0, 2, half, 0)


def project(s, r):
    cols, base = slice(r * 256, r * 256 + 256), r * 768
    x = s["x"][...].reshape(1024, 768)
    s["qkv"][:, base : base + 256] = dot(x, panel_of(s, 1 + r, 0, slice(0, 256))).astype(BF)
    for slot, half, off, scale, kept, at, factor in (
        (20, 0, 256, "scale_bv", "vt", 256, None),
        (8, 1, 0, "scale_bq", "qt", 512, SCALE_Q),
    ):
        low, high = (s["e"][slot + 2 * hb : slot + 2 * hb + 2].reshape(1024, 512) for hb in range(2))
        up = s["up_b"][r].reshape(1024, 256)
        t = dot(low, up[:512]) + dot(high, up[512:])
        s[kept][:, cols] = t.astype(BF)
        full = dot(x, panel_of(s, 1 + r, half, slice(off, off + 256))) + s[scale][:, cols] * t
        s["qkv"][:, base + at : base + at + 256] = (full * factor if factor else full).astype(BF)


def masks(s):
    def micro(m, _):
        pos = lax.broadcasted_iota(jnp.int32, (512, 128), 0)
        lane = lax.broadcasted_iota(jnp.int32, (512, 128), 1) % 64
        end = jnp.int32(0)
        pair = jnp.zeros((512, 128), jnp.int32)
        for p in range(4):
            end = end + s["parts"][m, 0, 2 * p] + s["parts"][m, 0, 2 * p + 1]
            pair = pair + (pos >= end).astype(jnp.int32)
        own = lane == pair
        s["mq"][m] = jnp.where(own, 1.0, 0.0).astype(BF)
        s["mk"][m] = jnp.where(own | (lane >= 8), 0.0, FAR).astype(BF)
        return 0

    lax.fori_loop(0, 2, micro, 0)


def places(r, i):
    m, half = i // 2, i % 2
    base = r * 768 + half * 128
    kvq = [span(base + j * 256, 128) for j in range(3)]
    return m, 2 * r + half, span(m * 512, 512), kvq, span(r * 256 + half * 128, 128)


def scores(s, buf, r, i, h):
    m, _, rows, (kc, _, qc), _ = places(r, i)
    mine = first_half() if h == 0 else ~first_half()
    k = jnp.where(mine, s["qkv"][rows, kc], s["mk"][m])
    q = jnp.where(mine, s["qkv"][rows, qc], s["mq"][m])
    buf[:, :512] = dot(q, k, NT)


def mix(s, buf, r, i, h):
    m, p, rows, (_, vc, _), _ = places(r, i)
    mine = first_half() if h == 0 else ~first_half()
    v = s["qkv"][rows, vc]
    sc = buf[:, :512]
    e = jnp.exp2(sc - jnp.max(sc, axis=1, keepdims=True)).astype(BF)
    s["e"][m * 12 + 2 * p + h] = e
    return dot(e, jnp.where(mine, v, jnp.ones_like(v)))


def attend(s, r):
    s_a, s_b = s["f_a"], s["g_one"].at[0:512, :]
    scores(s, s_a, r, 0, 0)

    def pair(i, _):
        _, _, rows, _, cols = places(r, i)
        scores(s, s_b, r, i, 1)
        o0 = mix(s, s_a, r, i, 0)
        scores(s, s_a, r, jnp.minimum(i + 1, 3), 0)
        o1 = mix(s, s_b, r, i, 1)
        total = pltpu.roll(jnp.where(first_half(), o1, o0), 64, 1)
        inverse = 1.0 / total
        s["inv"][rows, cols] = inverse.astype(BF)
        s["att"][rows, cols] = (jnp.where(first_half(), o0, o1) * inverse).astype(BF)
        return 0

    lax.fori_loop(0, 4, pair, 0, unroll=4)


def mean(v):
    return jnp.mean(v, axis=1, keepdims=True)


def norm(v):
    centred = v - mean(v)
    r = lax.rsqrt(mean(centred * centred) + 1e-05)
    return centred * r, r


def norm_back(hat, r, g):
    return r * (g - mean(g) - hat * mean(g * hat))


def by_rows(fn, size=128):
    for start in range(0, 512, size):
        fn(slice(start, start + size))


def middle(s, m, hooks=None):
    rows = span(m * 512, 512)
    hat, hid, slope = s["f_a"], s["hid"], s["slope"]
    other, low, inv = s["g_one"].at[rows, :], s["ga"].at[rows, :], s["inv"].at[rows, :]
    x, cot = s["x"].at[m], s["cot"].at[m]
    att = s["att"][rows, :]
    for r in range(3):
        hat[:, r * 256 : r * 256 + 256] = dot(att, panel_of(s, 1 + r, 1, slice(256, 512)))

    def norm_one(r):
        n, r1 = norm(x[r, :].astype(F32) + hat[r, :])
        hat[r, :] = n
        low[r, :] = (n * s["gain_one"][...] + s["shift_one"][...]).astype(BF)
        s["r1"][r, :] = r1

    by_rows(norm_one)

    if hooks:
        hooks[0]()
    for t in range(6):
        if hooks and t in hooks[2]:
            hooks[2][t]()
        u = dot(low[...], panel_of(s, 4 + t // 2, t % 2))
        cdf = 0.5 + 0.5 * lax.erf(u * 0.7071067811865476)
        cols = span(t * 512, 512)
        hid[:, cols] = (u * cdf).astype(BF)
        slope[:, cols] = (cdf + (u * 0.3989422804014327) * jnp.exp2(u * (u * (-0.5 * LOG2E)))).astype(BF)
    if hooks:
        hooks[1]()
    for k in range(3):
        other[:, k * 256 : k * 256 + 256] = dot(hid[...], s["down"][k].reshape(3072, 256))

    def norm_two(r):
        n2, r2 = norm(hat[r, :] * s["gain_one"][...] + s["shift_one"][...] + other[r, :])
        x[r, :] = (n2 * s["gain_two"][...] + s["shift_two"][...]).astype(BF)
        g = norm_back(n2, r2, cot[r, :].astype(F32) * s["gain_two"][...])
        other[r, :] = g
        low[r, :] = g.astype(BF)

    by_rows(norm_two)

    def back(t, _):
        cols = span(t * 768, 768)
        g = sum(dot(low[:, k * 256 : k * 256 + 256], s["down"][k, t // 2, t % 2].reshape(768, 256), NT) for k in range(3))
        hid[:, cols] = (g * slope[:, cols].astype(F32)).astype(BF)
        return 0

    lax.fori_loop(0, 4, back, 0, unroll=4)

    other[...] += sum(dot(hid[:, t * 512 : t * 512 + 512], panel_of(s, 4 + t // 2, t % 2), NT) for t in range(6))

    def norm_one_back(r):
        g = norm_back(hat[r, :], s["r1"][r, :], other[r, :] * s["gain_one"][...])
        other[r, :] = g
        low[r, :] = g.astype(BF)

    by_rows(norm_one_back)
    hat[...] = sum(dot(low[:, r * 256 : r * 256 + 256], panel_of(s, 1 + r, 1, slice(256, 512)), NT) for r in range(3))

    def scale_att(r):
        low[r, :] = (hat[r, :] * inv[r, :].astype(F32)).astype(BF)

    by_rows(scale_att)


def attend_back(s):
    def third(r, _):
        for i in range(4):
            m, p, rows, (kc, vc, qc), cols = places(r, i)
            k, v, q = s["qkv"][rows, kc], s["qkv"][rows, vc], s["qkv"][rows, qc]
            ga = s["ga"][rows, cols]
            prod = ga.astype(F32) * s["att"][rows, cols].astype(F32)
            gq = gk = gv = None
            lanes = lax.broadcasted_iota(jnp.int32, (1, 128), 1)
            for h in range(2):
                mine = first_half() if h == 0 else ~first_half()
                delta = -jnp.sum(jnp.where(mine, prod, 0.0), axis=1, keepdims=True)
                high = delta.astype(BF)
                rest = (delta - high.astype(F32)).astype(BF)
                zero = jnp.zeros_like(ga)
                gah = jnp.where(mine, ga, zero)
                aug = jnp.where(mine, ga, jnp.where(lanes % 64 == 0, high, jnp.where(lanes % 64 == 1, rest, zero)))
                gp = dot(aug, jnp.where(mine, v, jnp.ones_like(v)), NT)
                e = s["e"][m * 12 + 2 * p + h]
                gs = (e.astype(F32) * gp).astype(BF)
                gvh = dot(e, gah, TN)
                gqh = dot(gs, jnp.where(mine, k, zero))
                gkh = dot(gs, jnp.where(mine, q, zero), TN)
                gq, gk, gv = (gqh, gkh, gvh) if h == 0 else (gq + gqh, gk + gkh, gv + gvh)
            to = s[GRADS[m]]
            to[:, qc] = (gq * 0.125).astype(BF)
            to[:, kc] = (gk * (1.0 / LOG2E)).astype(BF)
            to[:, vc] = gv.astype(BF)
        return 0

    lax.fori_loop(0, 3, third, 0)


def vera_back(s):
    for base, kept, scale, row, keep in ((512, "qt", "scale_bq", 1, "att"), (256, "vt", "scale_bv", 3, "ga")):
        for r in range(3):
            cols = slice(r * 256, r * 256 + 256)

            total = jnp.zeros((1, 256), F32)
            for m in range(2):
                rows = slice(m * 512, m * 512 + 512)
                g = s[GRADS[m]][:, r * 768 + base : r * 768 + base + 256].astype(F32)
                s[keep][rows, cols] = (g * s[scale][:, cols]).astype(BF)
                total = total + jnp.sum(g * s[kept][rows, cols].astype(F32), axis=0, keepdims=True)
            s["red"][row : row + 1, cols] = total

    def half(hb, _):
        cols = span(hb * 512, 512)
        for m in range(2):
            rows = slice(m * 512, m * 512 + 512)
            gqu, gvu = (
                sum(dot(s[name][rows, r * 256 : r * 256 + 256], s["up_b"][r, hb].reshape(512, 256), NT) for r in range(3))
                for name in ("att", "ga")
            )
            lat = s["lat"][rows, cols].astype(F32)
            for row, val in ((0, gqu), (2, gvu)):
                part = jnp.sum(val * lat, axis=0, keepdims=True)
                if m:
                    part = part + s["red"][row : row + 1, cols]
                s["red"][row : row + 1, cols] = part
            s["e"][2 * hb + m] = (gqu * s["scale_dq"][:, cols] + gvu * s["scale_dv"][:, cols]).astype(BF)
        return 0

    lax.fori_loop(0, 2, half, 0)


def token_grads(s, m):
    rows = slice(m * 512, m * 512 + 512)
    terms = []
    for r in range(3):
        for j, (half, off) in enumerate(((0, 0), (0, 256), (1, 0))):
            lo = r * 768 + j * 256
            terms.append(dot(s[GRADS[m]][:, lo : lo + 256], panel_of(s, 1 + r, half, slice(off, off + 256)), NT))
    for hb in range(2):
        terms.append(dot(s["e"][2 * hb + m], panel_of(s, 0, hb), NT))
    s["cot"][m] = (s["g_one"][rows, :] + sum(terms)).astype(BF)


LAYER_SCRATCH = dict(
    panel=(PANEL, BF),
    down=(DOWN, BF),
    up_b=(UP_B, BF),
    x=((2, 512, 768), BF),
    cot=((2, 512, 768), BF),
    lat=((1024, 1024), BF),
    qt=((1024, 768), BF),
    vt=((1024, 768), BF),
    qkv=((1024, 2304), BF),
    e=((24, 512, 512), BF),
    att=((1024, 768), BF),
    inv=((1024, 768), BF),
    ga=((1024, 768), BF),
    g_one=((1024, 768), F32),
    f_a=((512, 768), F32),
    hid=((512, 3072), BF),
    slope=((512, 3072), BF),
    mq=((2, 512, 128), BF),
    mk=((2, 512, 128), BF),
    r1=((512, 1), F32),
    red=((4, 1024), F32),
)


VECTORS = ("gain_one", "shift_one", "gain_two", "shift_two", "scale_dq", "scale_bq", "scale_dv", "scale_bv")
SHARDS = ("w_query", "w_key", "w_value", "w_out", "w_up", "w_down", "shared_a", "shared_b")
SHARD_SHAPES = ((6, 768),) * 4 + ((6, 3072), (24, 768), (6, 1024), (8, 768))
GROUP_A, GROUP_1, GROUP_2, GROUP_3, UP_0, UP_1, UP_2 = (("panel", i, i + 1) for i in range(7))
DOWN_0, DOWN_1, DOWN_2 = (("down", i, i + 1) for i in range(3))
GROUP_B, FRONT, GROUP_UP, GROUP_DOWN = ("up_b", 0, 3), ("panel", 0, 4), ("panel", 4, 7), ("down", 0, 3)
LATE = (GROUP_UP, GROUP_DOWN)


def near_place(at):
    return (at["y"] % 2) * 4 + at["x"]


def across_place(at):
    return 8 + ((at["y"] // 2) * 2 + at["c"]) * 4 + at["z"]


def reduce_start(at, group, place_of, s, send, recv):
    here = place_of(at)
    s["sums"][pl.ds(here, 1)] = s["red"][...][None]
    sends, arrivals = [], []
    for i, other in enumerate(group(at)):
        k = i if place_of is near_place else 7 + i
        for found, slot in ((sends, here), (arrivals, place_of(other))):
            found.append(pltpu.make_async_remote_copy(
                src_ref=s["sums"].at[here], dst_ref=s["sums"].at[slot],
                send_sem=send.at[k], recv_sem=recv.at[place_of(other)] if found is arrivals else recv.at[here],
                device_id=device(other), device_id_type=MESH))
    for copy in sends:
        copy.start()
    return sends, arrivals


def reduce_end(state, first, size, s):
    sends, arrivals = state
    for copy in arrivals:
        copy.wait_recv()
    for copy in sends:
        copy.wait_send()
    values = [s["sums"][first + i] for i in range(size)]
    while len(values) > 1:
        values = [values[i] + values[i + 1] for i in range(0, len(values), 2)]
    s["red"][...] = values[0]


EXTRA = dict(
    packed=((8, 6, 896), BF),
    landed=((8, 6, 896), BF),
    half_d=((24, 384), BF),
    half_b=((8, 384), BF),
    both_b=((2, 8, 384), BF),
    both_d=((2, 24, 384), BF),
    rows=((48, 896), F32),
    sums=((24, 4, 1024), F32),
)


def whole(*refs):
    names = ("tokens", "parts_in", "cotangent") + tuple("in_" + n for n in SHARDS) + tuple("in_" + n for n in VECTORS)
    names += ("out", "grad_tokens", "grad_dq", "grad_bq", "grad_dv", "grad_bv")
    scratch = tuple(LAYER_SCRATCH) + tuple(EXTRA) + SHARDS + VECTORS
    names += scratch + ("parts", "loads", "send_0", "recv_0", "send", "recv", "send_r", "recv_r")
    s = dict(zip(names, refs, strict=True))
    at = place()
    enter_signal(at)
    loads = []
    pairs = [(s["in_" + n], s[n]) for n in SHARDS] + [(s["in_" + n], s[n].at[0]) for n in VECTORS]
    pairs += [(s["parts_in"], s["parts"]), (s["tokens"], s["x"]), (s["cotangent"], s["cot"])]
    for i, (src, dst) in enumerate(pairs):
        loads.append(pltpu.make_async_copy(src, dst, s["loads"].at[i]))
        loads[-1].start()
    for copy in loads[:8]:
        copy.wait()
    bufs = {k: s[k] for k in ("panel", "down", "up_b")}
    stage_zero(at, [s[n] for n in SHARDS], s["packed"], s["landed"], s["half_d"], s["half_b"], s["both_b"], s["both_d"], s["rows"], bufs, s["send_0"], s["recv_0"])
    moves = Moves(at, bufs, s["send"], s["recv"])
    begun = []

    def start(group, phase):
        moves.start(group, phase)
        begun.append((group, phase))

    def pass_on(group):
        moves.wait(group, 2)
        start(group, 3)

    def before_up():
        for group in (UP_0, UP_1, UP_2):
            moves.wait(group, 3)

    def before_down():
        for group in (DOWN_0, DOWN_1, DOWN_2):
            moves.wait(group, 3)

    hooks = (before_up, before_down, {i + 3: lambda g=g: pass_on(g) for i, g in enumerate((DOWN_0, DOWN_1, DOWN_2))})

    start(FRONT, 0)
    start(GROUP_B, 0)
    for group in LATE:
        start(group, 0)
    moves.wait(FRONT, 0)
    start(FRONT, 1)
    moves.wait(GROUP_B, 0)
    start(GROUP_B, 1)
    for group in LATE:
        moves.wait(group, 0)
        start(group, 1)
    moves.wait(FRONT, 1)
    start(GROUP_A, 2)
    start(GROUP_1, 2)
    moves.wait(GROUP_B, 1)
    start(GROUP_B, 2)
    start(GROUP_2, 2)
    for copy in loads[8:]:
        copy.wait()
    masks(s)
    pass_on(GROUP_A)
    start(GROUP_3, 2)
    moves.wait(GROUP_UP, 1)
    start(UP_0, 2)
    moves.wait(GROUP_A, 3)
    rank_down(s)
    pass_on(GROUP_1)
    pass_on(GROUP_B)
    start(UP_1, 2)
    start(UP_2, 2)
    moves.wait(GROUP_1, 3)
    moves.wait(GROUP_B, 3)
    project(s, 0)
    pass_on(GROUP_2)
    moves.wait(GROUP_DOWN, 1)
    start(DOWN_0, 2)
    attend(s, 0)
    pass_on(GROUP_3)
    start(DOWN_1, 2)
    moves.wait(GROUP_2, 3)
    project(s, 1)
    start(DOWN_2, 2)
    attend(s, 1)
    pass_on(UP_0)
    moves.wait(GROUP_3, 3)
    project(s, 2)
    pass_on(UP_1)
    attend(s, 2)
    pass_on(UP_2)
    middle(s, 0, hooks)
    middle(s, 1)
    result = pltpu.make_async_copy(s["x"], s["out"], s["loads"].at[0])
    result.start()
    for group, phase in begun:
        moves.sent(group, phase)
    attend_back(s)
    vera_back(s)
    for row in (1, 3):
        s["red"][row : row + 1, 768:1024] = jnp.zeros((1, 256), F32)
    state = reduce_start(at, near, near_place, s, s["send_r"], s["recv_r"])
    token_grads(s, 0)
    reduce_end(state, 0, 8, s)
    state = reduce_start(at, across, across_place, s, s["send_r"], s["recv_r"])
    token_grads(s, 1)
    ends = [result]
    ends.append(pltpu.make_async_copy(s["cot"], s["grad_tokens"], s["loads"].at[1]))
    ends[-1].start()
    reduce_end(state, 8, 16, s)
    for i, name in enumerate(("grad_dq", "grad_bq", "grad_dv", "grad_bv")):
        ends.append(pltpu.make_async_copy(s["red"].at[i, 0 : s[name].shape[0]], s[name], s["loads"].at[2 + i]))
        ends[-1].start()
    assert len(moves.slots) == 182
    assert len(moves.slots) == 182
    for copy in ends:
        copy.wait()


def hand_over(*refs):
    sources, results, held, sems = refs[:6], refs[6:12], refs[12:18], refs[18:]
    pieces = []
    for i, (src, dst, mid) in enumerate(zip(sources, results, held, strict=True)):
        if i < 2:
            pieces += [[a.at[m, r : r + 256] for a in (src, mid, dst)] for m in range(2) for r in (0, 256)]
        else:
            pieces.append([src, mid, dst])
    ins = [pltpu.make_async_copy(a, b, sems[0].at[k]) for k, (a, b, _) in enumerate(pieces)]
    outs = [pltpu.make_async_copy(b, c, sems[1].at[k]) for k, (_, b, c) in enumerate(pieces)]
    for copy in ins:
        copy.start()
    for before, after in zip(ins, outs, strict=True):
        before.wait()
        after.start()
    for copy in outs:
        copy.wait()


def shards(tokens, parts, cotangent, *rest):
    anywhere = pl.BlockSpec(memory_space=pl.ANY)
    scratch = [pltpu.VMEM(shape, kind) for shape, kind in (*LAYER_SCRATCH.values(), *EXTRA.values())]
    scratch += [pltpu.VMEM(shape, BF) for shape in SHARD_SHAPES]
    scratch += [pltpu.VMEM((1, v.shape[0]), F32) for v in rest[8:]]
    scratch += [pltpu.SMEM((2, 1, 8), jnp.int32)]
    scratch += [pltpu.SemaphoreType.DMA((n,)) for n in (19, 10, 10, 182, 182, 22, 24)]
    shapes = [jax.ShapeDtypeStruct((2, 512, 768), BF)] * 2
    shapes += [jax.ShapeDtypeStruct((n,), F32) for n in (1024, 768, 1024, 768)]
    found = pl.pallas_call(
        whole,
        out_shape=shapes,
        in_specs=[anywhere] * 19,
        out_specs=[anywhere] * 6,
        scratch_shapes=scratch,
        compiler_params=pltpu.CompilerParams(collective_id=0, has_side_effects=True, vmem_limit_bytes=66900000),
    )(tokens, parts, cotangent, *rest)
    held = [pltpu.VMEM(shape.shape, shape.dtype) for shape in shapes]
    return tuple(pl.pallas_call(
        hand_over,
        out_shape=shapes,
        in_specs=[anywhere] * 6,
        out_specs=[anywhere] * 6,
        scratch_shapes=held + [pltpu.SemaphoreType.DMA((12,))] * 2,
        compiler_params=pltpu.CompilerParams(vmem_limit_bytes=8 << 20),
    )(*found))


def solution(mesh):
    rows, split, same = P(None, ("dp", "fsdp"), None), P(("dp", "fsdp"), None), P()
    return jax.shard_map(
        shards,
        mesh=mesh,
        in_specs=(rows,) * 3 + (split,) * 8 + (same,) * 8,
        out_specs=(rows, rows, same, same, same, same),
        check_vma=False,
    )
```

```python
import jax
import jax.numpy as jnp
from jax import lax
from jax.experimental import pallas as pl
from jax.experimental.pallas import tpu as pltpu
from jax.sharding import PartitionSpec as P

MESH = pl.DeviceIdType.MESH
BF = jnp.bfloat16
F32 = jnp.float32


def place():
    dp = lax.axis_index("dp")
    fs = lax.axis_index("fsdp")
    return dict(x=fs % 4, y=(dp // 2) * 2 + (fs // 4) % 2, z=fs // 8, c=dp % 2)


def device(at):
    return ((at["y"] // 2) * 2 + at["c"], at["z"] * 8 + (at["y"] % 2) * 4 + at["x"])


def moved(at, axis, delta):
    size = 2 if axis == "c" else 4
    return {**at, axis: (at[axis] + delta + size) % size}


ORDERS = (("x", "y", "z"), ("y", "z", "x"), ("z", "x", "y"))
PEERS = 23


def near(at):
    for step in range(1, 8):
        x, yl = (at["x"] + step) % 4, (at["y"] + step // 4) % 2
        yield {**at, "x": x, "y": (at["y"] // 2) * 2 + yl}


def across(at):
    for step in range(1, 16):
        yh, c = (at["y"] // 2 + step // 8) % 2, (at["c"] + step // 4) % 2
        yield {**at, "y": yh * 2 + at["y"] % 2, "c": c, "z": (at["z"] + step) % 4}


def peers(at):
    return [*near(at), *across(at), {**at, "y": 3 - at["y"]}]


def enter_signal(at):
    for peer in peers(at):
        pl.semaphore_signal(pltpu.get_barrier_semaphore(), inc=1, device_id=device(peer), device_id_type=MESH)


def region(buf, kind, rot, done, at, low, high):
    every = slice(None)
    x, y, z, c = at["x"], at["y"], at["z"], at["c"]
    yh = every if "y" in done else y // 2
    yl = every if "y" in done else y % 2
    zs = every if "z" in done else z
    col = every if "x" in done else pl.ds(pl.multiple_of(x * 128, 128), 128)
    if kind == "panel":
        return buf.at[low:high, yl, yh, c, zs, rot, :, col]
    col = every if "x" in done else pl.ds(pl.multiple_of((x % 2) * 128, 128), 128)
    xh = every if "x" in done else x // 2
    if kind == "down":
        return buf.at[low:high, yh, c, zs, yl, xh, rot, :, col]
    return buf.at[rot, yh, c, zs, yl, xh, :, col]


class Moves:
    def __init__(self, at, bufs, send, recv):
        self.at, self.bufs, self.send, self.recv = at, bufs, send, recv
        self.slots = {}

    def slot(self, key):
        return self.slots.setdefault(key, len(self.slots))

    def copies(self, group, phase):
        kind, low, high = group
        buf = self.bufs[kind]
        for rot in range(3):
            order = ORDERS[rot]
            axis, done = order[phase], order[:phase]
            for delta in (2, 1, 3):
                k = self.slot((group, phase, rot, delta))
                yield (
                    region(buf, kind, rot, done, self.at, low, high),
                    moved(self.at, axis, delta),
                    region(buf, kind, rot, done, moved(self.at, axis, -delta), low, high),
                    k,
                )

    def sibling(self, group):
        kind, low, high = group
        buf = self.bufs[kind]
        k = self.slot((group, "c"))
        for here in (self.at,):
            other = moved(here, "c", 1)
            if kind == "panel":
                mine, theirs = buf.at[low:high, :, :, here["c"]], buf.at[low:high, :, :, other["c"]]
            elif kind == "up_b":
                mine, theirs = buf.at[:, :, here["c"]], buf.at[:, :, other["c"]]
            else:
                mine, theirs = buf.at[low:high, :, here["c"]], buf.at[low:high, :, other["c"]]
            yield mine, other, theirs, k

    def make(self, what):
        mine, target, theirs, k = what
        return pltpu.make_async_remote_copy(
            src_ref=mine,
            dst_ref=mine,
            send_sem=self.send.at[k],
            recv_sem=self.recv.at[k],
            device_id=device(target),
            device_id_type=MESH,
        )

    def arrival(self, what):
        mine, target, theirs, k = what
        return pltpu.make_async_remote_copy(
            src_ref=theirs,
            dst_ref=theirs,
            send_sem=self.send.at[k],
            recv_sem=self.recv.at[k],
            device_id=device(target),
            device_id_type=MESH,
        )

    def listed(self, group, phase):
        return self.sibling(group) if phase == 3 else self.copies(group, phase)

    def start(self, group, phase):
        for what in self.listed(group, phase):
            self.make(what).start()

    def wait(self, group, phase):
        for what in self.listed(group, phase):
            self.arrival(what).wait_recv()

    def sent(self, group, phase):
        for what in self.listed(group, phase):
            self.make(what).wait_send()


def stage_zero(at, shards, packed, landed, half_d, half_b, both_b, both_d, rows, bufs, send, recv):
    w_query, w_key, w_value, w_out, w_up, w_down, shared_a, shared_b = shards
    kvqo = (w_key, w_value, w_query, w_out)
    x, y, z, c = at["x"], at["y"], at["z"], at["c"]
    mine = (y % 2) * 4 + x

    def pick(ch, yl, dx):
        col = yl * 512 + dx * 128
        if ch == 0:
            return shared_a[:, col : col + 128]
        if ch < 4:
            start = (ch - 1) * 256 + col % 256
            return kvqo[col // 256][:, start : start + 128]
        start = (ch - 4) * 1024 + col
        return w_up[:, start : start + 128]

    for yl in range(2):
        for dx in range(4):
            for ch in range(7):
                packed[yl * 4 + dx, :, ch * 128 : ch * 128 + 128] = pick(ch, yl, dx)
    for odd in range(2):
        for r in range(3):
            tile = slice(r * 256 + odd * 128, r * 256 + odd * 128 + 128)
            both_b[odd, :, r * 128 : r * 128 + 128] = shared_b[:, tile]
            both_d[odd, :, r * 128 : r * 128 + 128] = w_down[:, tile]
    landed[pl.ds(mine, 1)] = packed[pl.ds(mine, 1)]
    pl.semaphore_wait(pltpu.get_barrier_semaphore(), PEERS)
    sends, arrivals = [], []
    for step in range(1, 8):
        dx, dy = step % 4, step // 4
        to = {**at, "x": (x + dx) % 4, "y": (y // 2) * 2 + (y + dy) % 2}
        fro = {**at, "x": (x - dx + 4) % 4, "y": (y // 2) * 2 + (y + dy) % 2}
        to_i, fro_i = (to["y"] % 2) * 4 + to["x"], (fro["y"] % 2) * 4 + fro["x"]
        sends.append(pltpu.make_async_remote_copy(
            src_ref=packed.at[to_i], dst_ref=landed.at[mine], send_sem=send.at[step], recv_sem=recv.at[step],
            device_id=device(to), device_id_type=MESH))
        arrivals.append(pltpu.make_async_remote_copy(
            src_ref=packed.at[to_i], dst_ref=landed.at[fro_i], send_sem=send.at[step], recv_sem=recv.at[step],
            device_id=device(to), device_id_type=MESH))
    other = {**at, "x": x + 1 - 2 * (x % 2)}
    for k, (src, dst) in enumerate(((both_d.at[1 - x % 2], half_d), (both_b.at[1 - x % 2], half_b))):
        sends.append(pltpu.make_async_remote_copy(
            src_ref=src, dst_ref=dst, send_sem=send.at[8 + k], recv_sem=recv.at[8 + k],
            device_id=device(other), device_id_type=MESH))
        arrivals.append(sends[-1])
    for copy in sends:
        copy.start()
    for copy in arrivals:
        copy.wait_recv()
    for i in range(8):
        rows[6 * i : 6 * i + 6, :] = landed[i].astype(F32)
    yh, yl = y // 2, y % 2
    block = rows[...].astype(BF).reshape(3, 16, 896)
    own = pl.ds(pl.multiple_of(x * 128, 128), 128)
    for ch in range(7):
        bufs["panel"][ch, yl, yh, c, z, :, :, own] = block[:, :, ch * 128 : ch * 128 + 128]
    lane = pl.ds(pl.multiple_of((x % 2) * 128, 128), 128)

    def joined(mine_too, got):
        a, b = mine_too.astype(F32), got[...].astype(F32)
        even = x % 2 == 0
        return jnp.concatenate([jnp.where(even, a, b), jnp.where(even, b, a)], axis=0).astype(BF)

    block = joined(both_d[x % 2], half_d).reshape(3, 16, 384)
    for k in range(3):
        bufs["down"][k, yh, c, z, yl, x // 2, :, :, lane] = block[:, :, k * 128 : k * 128 + 128]
    pair = joined(both_b[x % 2], half_b)
    for r in range(3):
        bufs["up_b"][r, yh, c, z, yl, x // 2, :, lane] = pair[:, r * 128 : r * 128 + 128]
    for copy in sends:
        copy.wait_send()


PANEL = (7, 2, 2, 2, 4, 3, 16, 512)
DOWN = (3, 2, 2, 4, 2, 2, 3, 16, 256)
UP_B = (3, 2, 2, 4, 2, 2, 16, 256)


LOG2E = 1.4426950408889634
SCALE_Q = 0.125 * LOG2E
NT = (((1,), (1,)), ((), ()))
TN = (((0,), (0,)), ((), ()))
NN = (((1,), (0,)), ((), ()))
FAR = -1e30
GRADS = ("hid", "slope")


def dot(left, right, dims=NN):
    return lax.dot_general(left, right, dims, preferred_element_type=F32)


def span(start, size):
    return pl.ds(pl.multiple_of(start, size), size)


def panel_of(s, ch, half, cols=slice(None)):
    part = s["panel"][ch, half, :, :, :, :, :, cols]
    return part.reshape(768, part.shape[-1])


def first_half(width=128):
    return lax.broadcasted_iota(jnp.int32, (1, width), 1) < 64


def rank_down(s):
    def half(hb, _):
        cols = span(hb * 512, 512)
        lat = dot(s["x"][...].reshape(1024, 768), panel_of(s, 0, hb))
        s["lat"][:, cols] = lat.astype(BF)
        for slot, name in ((8, "scale_dq"), (20, "scale_dv")):
            s["e"][pl.ds(slot + 2 * hb, 2)] = (lat * s[name][:, cols]).astype(BF).reshape(2, 512, 512)
        return 0

    lax.fori_loop(0, 2, half, 0)


def project(s, r):
    cols, base = slice(r * 256, r * 256 + 256), r * 768
    x = s["x"][...].reshape(1024, 768)
    s["qkv"][:, base : base + 256] = dot(x, panel_of(s, 1 + r, 0, slice(0, 256))).astype(BF)
    for slot, half, off, scale, kept, at, factor in (
        (20, 0, 256, "scale_bv", "vt", 256, None),
        (8, 1, 0, "scale_bq", "qt", 512, SCALE_Q),
    ):
        low, high = (s["e"][slot + 2 * hb : slot + 2 * hb + 2].reshape(1024, 512) for hb in range(2))
        up = s["up_b"][r].reshape(1024, 256)
        t = dot(low, up[:512]) + dot(high, up[512:])
        s[kept][:, cols] = t.astype(BF)
        full = dot(x, panel_of(s, 1 + r, half, slice(off, off + 256))) + s[scale][:, cols] * t
        s["qkv"][:, base + at : base + at + 256] = (full * factor if factor else full).astype(BF)


def masks(s):
    def micro(m, _):
        pos = lax.broadcasted_iota(jnp.int32, (512, 128), 0)
        lane = lax.broadcasted_iota(jnp.int32, (512, 128), 1) % 64
        end = jnp.int32(0)
        pair = jnp.zeros((512, 128), jnp.int32)
        for p in range(4):
            end = end + s["parts"][m, 0, 2 * p] + s["parts"][m, 0, 2 * p + 1]
            pair = pair + (pos >= end).astype(jnp.int32)
        own = lane == pair
        s["mq"][m] = jnp.where(own, 1.0, 0.0).astype(BF)
        s["mk"][m] = jnp.where(own | (lane >= 8), 0.0, FAR).astype(BF)
        return 0

    lax.fori_loop(0, 2, micro, 0)


def places(r, i):
    m, half = i // 2, i % 2
    base = r * 768 + half * 128
    kvq = [span(base + j * 256, 128) for j in range(3)]
    return m, 2 * r + half, span(m * 512, 512), kvq, span(r * 256 + half * 128, 128)


def scores(s, buf, r, i, h):
    m, _, rows, (kc, _, qc), _ = places(r, i)
    mine = first_half() if h == 0 else ~first_half()
    k = jnp.where(mine, s["qkv"][rows, kc], s["mk"][m])
    q = jnp.where(mine, s["qkv"][rows, qc], s["mq"][m])
    buf[:, :512] = dot(q, k, NT)


def mix(s, buf, r, i, h):
    m, p, rows, (_, vc, _), _ = places(r, i)
    mine = first_half() if h == 0 else ~first_half()
    v = s["qkv"][rows, vc]
    sc = buf[:, :512]
    e = jnp.exp2(sc - jnp.max(sc, axis=1, keepdims=True)).astype(BF)
    s["e"][m * 12 + 2 * p + h] = e
    return dot(e, jnp.where(mine, v, jnp.ones_like(v)))


def attend(s, r):
    s_a, s_b = s["f_a"], s["g_one"].at[0:512, :]
    scores(s, s_a, r, 0, 0)

    def pair(i, _):
        _, _, rows, _, cols = places(r, i)
        scores(s, s_b, r, i, 1)
        o0 = mix(s, s_a, r, i, 0)
        scores(s, s_a, r, jnp.minimum(i + 1, 3), 0)
        o1 = mix(s, s_b, r, i, 1)
        total = pltpu.roll(jnp.where(first_half(), o1, o0), 64, 1)
        inverse = 1.0 / total
        s["inv"][rows, cols] = inverse.astype(BF)
        s["att"][rows, cols] = (jnp.where(first_half(), o0, o1) * inverse).astype(BF)
        return 0

    lax.fori_loop(0, 4, pair, 0, unroll=4)


def mean(v):
    return jnp.mean(v, axis=1, keepdims=True)


def norm(v):
    centred = v - mean(v)
    r = lax.rsqrt(mean(centred * centred) + 1e-05)
    return centred * r, r


def norm_back(hat, r, g):
    return r * (g - mean(g) - hat * mean(g * hat))


def by_rows(fn, size=128):
    for start in range(0, 512, size):
        fn(slice(start, start + size))


def middle(s, m, hooks=None):
    rows = span(m * 512, 512)
    hat, hid, slope = s["f_a"], s["hid"], s["slope"]
    other, low, inv = s["g_one"].at[rows, :], s["ga"].at[rows, :], s["inv"].at[rows, :]
    x, cot = s["x"].at[m], s["cot"].at[m]
    att = s["att"][rows, :]
    for r in range(3):
        hat[:, r * 256 : r * 256 + 256] = dot(att, panel_of(s, 1 + r, 1, slice(256, 512)))

    def norm_one(r):
        n, r1 = norm(x[r, :].astype(F32) + hat[r, :])
        hat[r, :] = n
        low[r, :] = (n * s["gain_one"][...] + s["shift_one"][...]).astype(BF)
        s["r1"][r, :] = r1

    by_rows(norm_one)

    if hooks:
        hooks[0]()
    for t in range(6):
        if hooks and t in hooks[2]:
            hooks[2][t]()
        u = dot(low[...], panel_of(s, 4 + t // 2, t % 2))
        cdf = 0.5 + 0.5 * lax.erf(u * 0.7071067811865476)
        cols = span(t * 512, 512)
        hid[:, cols] = (u * cdf).astype(BF)
        slope[:, cols] = (cdf + (u * 0.3989422804014327) * jnp.exp2(u * (u * (-0.5 * LOG2E)))).astype(BF)
    if hooks:
        hooks[1]()
    for k in range(3):
        other[:, k * 256 : k * 256 + 256] = dot(hid[...], s["down"][k].reshape(3072, 256))

    def norm_two(r):
        n2, r2 = norm(hat[r, :] * s["gain_one"][...] + s["shift_one"][...] + other[r, :])
        x[r, :] = (n2 * s["gain_two"][...] + s["shift_two"][...]).astype(BF)
        g = norm_back(n2, r2, cot[r, :].astype(F32) * s["gain_two"][...])
        other[r, :] = g
        low[r, :] = g.astype(BF)

    by_rows(norm_two)

    def back(t, _):
        cols = span(t * 768, 768)
        g = sum(dot(low[:, k * 256 : k * 256 + 256], s["down"][k, t // 2, t % 2].reshape(768, 256), NT) for k in range(3))
        hid[:, cols] = (g * slope[:, cols].astype(F32)).astype(BF)
        return 0

    lax.fori_loop(0, 4, back, 0, unroll=4)

    other[...] += sum(dot(hid[:, t * 512 : t * 512 + 512], panel_of(s, 4 + t // 2, t % 2), NT) for t in range(6))

    def norm_one_back(r):
        g = norm_back(hat[r, :], s["r1"][r, :], other[r, :] * s["gain_one"][...])
        other[r, :] = g
        low[r, :] = g.astype(BF)

    by_rows(norm_one_back)
    hat[...] = sum(dot(low[:, r * 256 : r * 256 + 256], panel_of(s, 1 + r, 1, slice(256, 512)), NT) for r in range(3))

    def scale_att(r):
        low[r, :] = (hat[r, :] * inv[r, :].astype(F32)).astype(BF)

    by_rows(scale_att)


def attend_back(s):
    def third(r, _):
        for i in range(4):
            m, p, rows, (kc, vc, qc), cols = places(r, i)
            k, v, q = s["qkv"][rows, kc], s["qkv"][rows, vc], s["qkv"][rows, qc]
            ga = s["ga"][rows, cols]
            prod = ga.astype(F32) * s["att"][rows, cols].astype(F32)
            gq = gk = gv = None
            lanes = lax.broadcasted_iota(jnp.int32, (1, 128), 1)
            for h in range(2):
                mine = first_half() if h == 0 else ~first_half()
                delta = -jnp.sum(jnp.where(mine, prod, 0.0), axis=1, keepdims=True)
                high = delta.astype(BF)
                rest = (delta - high.astype(F32)).astype(BF)
                zero = jnp.zeros_like(ga)
                gah = jnp.where(mine, ga, zero)
                aug = jnp.where(mine, ga, jnp.where(lanes % 64 == 0, high, jnp.where(lanes % 64 == 1, rest, zero)))
                gp = dot(aug, jnp.where(mine, v, jnp.ones_like(v)), NT)
                e = s["e"][m * 12 + 2 * p + h]
                gs = (e.astype(F32) * gp).astype(BF)
                gvh = dot(e, gah, TN)
                gqh = dot(gs, jnp.where(mine, k, zero))
                gkh = dot(gs, jnp.where(mine, q, zero), TN)
                gq, gk, gv = (gqh, gkh, gvh) if h == 0 else (gq + gqh, gk + gkh, gv + gvh)
            to = s[GRADS[m]]
            to[:, qc] = (gq * 0.125).astype(BF)
            to[:, kc] = (gk * (1.0 / LOG2E)).astype(BF)
            to[:, vc] = gv.astype(BF)
        return 0

    lax.fori_loop(0, 3, third, 0)


def vera_back(s):
    for base, kept, scale, row, keep in ((512, "qt", "scale_bq", 1, "att"), (256, "vt", "scale_bv", 3, "ga")):
        for r in range(3):
            cols = slice(r * 256, r * 256 + 256)

            total = jnp.zeros((1, 256), F32)
            for m in range(2):
                rows = slice(m * 512, m * 512 + 512)
                g = s[GRADS[m]][:, r * 768 + base : r * 768 + base + 256].astype(F32)
                s[keep][rows, cols] = (g * s[scale][:, cols]).astype(BF)
                total = total + jnp.sum(g * s[kept][rows, cols].astype(F32), axis=0, keepdims=True)
            s["red"][row : row + 1, cols] = total

    def half(hb, _):
        cols = span(hb * 512, 512)
        for m in range(2):
            rows = slice(m * 512, m * 512 + 512)
            gqu, gvu = (
                sum(dot(s[name][rows, r * 256 : r * 256 + 256], s["up_b"][r, hb].reshape(512, 256), NT) for r in range(3))
                for name in ("att", "ga")
            )
            lat = s["lat"][rows, cols].astype(F32)
            for row, val in ((0, gqu), (2, gvu)):
                part = jnp.sum(val * lat, axis=0, keepdims=True)
                if m:
                    part = part + s["red"][row : row + 1, cols]
                s["red"][row : row + 1, cols] = part
            s["e"][2 * hb + m] = (gqu * s["scale_dq"][:, cols] + gvu * s["scale_dv"][:, cols]).astype(BF)
        return 0

    lax.fori_loop(0, 2, half, 0)


def token_grads(s, m):
    rows = slice(m * 512, m * 512 + 512)
    terms = []
    for r in range(3):
        for j, (half, off) in enumerate(((0, 0), (0, 256), (1, 0))):
            lo = r * 768 + j * 256
            terms.append(dot(s[GRADS[m]][:, lo : lo + 256], panel_of(s, 1 + r, half, slice(off, off + 256)), NT))
    for hb in range(2):
        terms.append(dot(s["e"][2 * hb + m], panel_of(s, 0, hb), NT))
    s["cot"][m] = (s["g_one"][rows, :] + sum(terms)).astype(BF)


LAYER_SCRATCH = dict(
    panel=(PANEL, BF),
    down=(DOWN, BF),
    up_b=(UP_B, BF),
    x=((2, 512, 768), BF),
    cot=((2, 512, 768), BF),
    lat=((1024, 1024), BF),
    qt=((1024, 768), BF),
    vt=((1024, 768), BF),
    qkv=((1024, 2304), BF),
    e=((24, 512, 512), BF),
    att=((1024, 768), BF),
    inv=((1024, 768), BF),
    ga=((1024, 768), BF),
    g_one=((1024, 768), F32),
    f_a=((512, 768), F32),
    hid=((512, 3072), BF),
    slope=((512, 3072), BF),
    mq=((2, 512, 128), BF),
    mk=((2, 512, 128), BF),
    r1=((512, 1), F32),
    red=((4, 1024), F32),
)


VECTORS = ("gain_one", "shift_one", "gain_two", "shift_two", "scale_dq", "scale_bq", "scale_dv", "scale_bv")
SHARDS = ("w_query", "w_key", "w_value", "w_out", "w_up", "w_down", "shared_a", "shared_b")
SHARD_SHAPES = ((6, 768),) * 4 + ((6, 3072), (24, 768), (6, 1024), (8, 768))
GROUP_A, GROUP_1, GROUP_2, GROUP_3, UP_0, UP_1, UP_2 = (("panel", i, i + 1) for i in range(7))
DOWN_0, DOWN_1, DOWN_2 = (("down", i, i + 1) for i in range(3))
GROUP_B, FRONT, GROUP_UP, GROUP_DOWN = ("up_b", 0, 3), ("panel", 0, 4), ("panel", 4, 7), ("down", 0, 3)
LATE = (GROUP_UP, GROUP_DOWN)


def near_place(at):
    return (at["y"] % 2) * 4 + at["x"]


def across_place(at):
    return 8 + ((at["y"] // 2) * 2 + at["c"]) * 4 + at["z"]


def reduce_start(at, group, place_of, s, send, recv):
    here = place_of(at)
    s["sums"][pl.ds(here, 1)] = s["red"][...][None]
    sends, arrivals = [], []
    for i, other in enumerate(group(at)):
        k = i if place_of is near_place else 7 + i
        for found, slot in ((sends, here), (arrivals, place_of(other))):
            found.append(pltpu.make_async_remote_copy(
                src_ref=s["sums"].at[here], dst_ref=s["sums"].at[slot],
                send_sem=send.at[k], recv_sem=recv.at[place_of(other)] if found is arrivals else recv.at[here],
                device_id=device(other), device_id_type=MESH))
    for copy in sends:
        copy.start()
    return sends, arrivals


def reduce_end(state, first, size, s):
    sends, arrivals = state
    for copy in arrivals:
        copy.wait_recv()
    for copy in sends:
        copy.wait_send()
    values = [s["sums"][first + i] for i in range(size)]
    while len(values) > 1:
        values = [values[i] + values[i + 1] for i in range(0, len(values), 2)]
    s["red"][...] = values[0]


EXTRA = dict(
    packed=((8, 6, 896), BF),
    landed=((8, 6, 896), BF),
    half_d=((24, 384), BF),
    half_b=((8, 384), BF),
    both_b=((2, 8, 384), BF),
    both_d=((2, 24, 384), BF),
    rows=((48, 896), F32),
    sums=((24, 4, 1024), F32),
)


def whole(*refs):
    names = ("tokens", "parts_in", "cotangent") + tuple("in_" + n for n in SHARDS) + tuple("in_" + n for n in VECTORS)
    names += ("out", "grad_tokens", "grad_dq", "grad_bq", "grad_dv", "grad_bv")
    scratch = tuple(LAYER_SCRATCH) + tuple(EXTRA) + SHARDS + VECTORS
    names += scratch + ("parts", "loads", "send_0", "recv_0", "send", "recv", "send_r", "recv_r")
    s = dict(zip(names, refs, strict=True))
    at = place()
    enter_signal(at)
    loads = []
    pairs = [(s["in_" + n], s[n]) for n in SHARDS] + [(s["in_" + n], s[n].at[0]) for n in VECTORS]
    pairs += [(s["parts_in"], s["parts"]), (s["tokens"], s["x"]), (s["cotangent"], s["cot"])]
    for i, (src, dst) in enumerate(pairs):
        loads.append(pltpu.make_async_copy(src, dst, s["loads"].at[i]))
        loads[-1].start()
    for copy in loads[:8]:
        copy.wait()
    bufs = {k: s[k] for k in ("panel", "down", "up_b")}
    stage_zero(at, [s[n] for n in SHARDS], s["packed"], s["landed"], s["half_d"], s["half_b"], s["both_b"], s["both_d"], s["rows"], bufs, s["send_0"], s["recv_0"])
    moves = Moves(at, bufs, s["send"], s["recv"])
    begun = []

    def start(group, phase):
        moves.start(group, phase)
        begun.append((group, phase))

    def pass_on(group):
        moves.wait(group, 2)
        start(group, 3)

    def before_up():
        for group in (UP_0, UP_1, UP_2):
            moves.wait(group, 3)

    def before_down():
        for group in (DOWN_0, DOWN_1, DOWN_2):
            moves.wait(group, 3)

    hooks = (before_up, before_down, {i + 3: lambda g=g: pass_on(g) for i, g in enumerate((DOWN_0, DOWN_1, DOWN_2))})

    start(FRONT, 0)
    start(GROUP_B, 0)
    for group in LATE:
        start(group, 0)
    moves.wait(FRONT, 0)
    start(FRONT, 1)
    moves.wait(GROUP_B, 0)
    start(GROUP_B, 1)
    for group in LATE:
        moves.wait(group, 0)
        start(group, 1)
    moves.wait(FRONT, 1)
    start(GROUP_A, 2)
    start(GROUP_1, 2)
    moves.wait(GROUP_B, 1)
    start(GROUP_B, 2)
    start(GROUP_2, 2)
    for copy in loads[8:]:
        copy.wait()
    masks(s)
    pass_on(GROUP_A)
    start(GROUP_3, 2)
    moves.wait(GROUP_UP, 1)
    start(UP_0, 2)
    moves.wait(GROUP_A, 3)
    rank_down(s)
    pass_on(GROUP_1)
    pass_on(GROUP_B)
    start(UP_1, 2)
    start(UP_2, 2)
    moves.wait(GROUP_1, 3)
    moves.wait(GROUP_B, 3)
    project(s, 0)
    pass_on(GROUP_2)
    moves.wait(GROUP_DOWN, 1)
    start(DOWN_0, 2)
    attend(s, 0)
    pass_on(GROUP_3)
    start(DOWN_1, 2)
    moves.wait(GROUP_2, 3)
    project(s, 1)
    start(DOWN_2, 2)
    attend(s, 1)
    pass_on(UP_0)
    moves.wait(GROUP_3, 3)
    project(s, 2)
    pass_on(UP_1)
    attend(s, 2)
    pass_on(UP_2)
    middle(s, 0, hooks)
    middle(s, 1)
    result = pltpu.make_async_copy(s["x"], s["out"], s["loads"].at[0])
    result.start()
    for group, phase in begun:
        moves.sent(group, phase)
    attend_back(s)
    vera_back(s)
    for row in (1, 3):
        s["red"][row : row + 1, 768:1024] = jnp.zeros((1, 256), F32)
    state = reduce_start(at, near, near_place, s, s["send_r"], s["recv_r"])
    token_grads(s, 0)
    ends = [result]
    ends.append(pltpu.make_async_copy(s["cot"].at[0], s["grad_tokens"].at[0], s["loads"].at[1]))
    ends[-1].start()
    reduce_end(state, 0, 8, s)
    state = reduce_start(at, across, across_place, s, s["send_r"], s["recv_r"])
    token_grads(s, 1)
    ends.append(pltpu.make_async_copy(s["cot"].at[1], s["grad_tokens"].at[1], s["loads"].at[6]))
    ends[-1].start()
    reduce_end(state, 8, 16, s)
    for i, name in enumerate(("grad_dq", "grad_bq", "grad_dv", "grad_bv")):
        ends.append(pltpu.make_async_copy(s["red"].at[i, 0 : s[name].shape[0]], s[name], s["loads"].at[2 + i]))
        ends[-1].start()
    assert len(moves.slots) == 182
    assert len(moves.slots) == 182
    for copy in ends:
        copy.wait()


def hand_over(*refs):
    sources, results, held, sems = refs[:6], refs[6:12], refs[12:18], refs[18:]
    pieces = []
    for i, (src, dst, mid) in enumerate(zip(sources, results, held, strict=True)):
        if i < 2:
            pieces += [[a.at[m, r : r + 256] for a in (src, mid, dst)] for m in range(2) for r in (0, 256)]
        else:
            pieces.append([src, mid, dst])
    ins = [pltpu.make_async_copy(a, b, sems[0].at[k]) for k, (a, b, _) in enumerate(pieces)]
    outs = [pltpu.make_async_copy(b, c, sems[1].at[k]) for k, (_, b, c) in enumerate(pieces)]
    for copy in ins:
        copy.start()
    for before, after in zip(ins, outs, strict=True):
        before.wait()
        after.start()
    for copy in outs:
        copy.wait()


def shards(tokens, parts, cotangent, *rest):
    anywhere = pl.BlockSpec(memory_space=pl.ANY)
    scratch = [pltpu.VMEM(shape, kind) for shape, kind in (*LAYER_SCRATCH.values(), *EXTRA.values())]
    scratch += [pltpu.VMEM(shape, BF) for shape in SHARD_SHAPES]
    scratch += [pltpu.VMEM((1, v.shape[0]), F32) for v in rest[8:]]
    scratch += [pltpu.SMEM((2, 1, 8), jnp.int32)]
    scratch += [pltpu.SemaphoreType.DMA((n,)) for n in (19, 10, 10, 182, 182, 22, 24)]
    shapes = [jax.ShapeDtypeStruct((2, 512, 768), BF)] * 2
    shapes += [jax.ShapeDtypeStruct((n,), F32) for n in (1024, 768, 1024, 768)]
    found = pl.pallas_call(
        whole,
        out_shape=shapes,
        in_specs=[anywhere] * 19,
        out_specs=[anywhere] * 6,
        scratch_shapes=scratch,
        compiler_params=pltpu.CompilerParams(collective_id=0, has_side_effects=True, vmem_limit_bytes=66900000),
    )(tokens, parts, cotangent, *rest)
    held = [pltpu.VMEM(shape.shape, shape.dtype) for shape in shapes]
    return tuple(pl.pallas_call(
        hand_over,
        out_shape=shapes,
        in_specs=[anywhere] * 6,
        out_specs=[anywhere] * 6,
        scratch_shapes=held + [pltpu.SemaphoreType.DMA((12,))] * 2,
        compiler_params=pltpu.CompilerParams(vmem_limit_bytes=66900000),
    )(*found))


def solution(mesh):
    rows, split, same = P(None, ("dp", "fsdp"), None), P(("dp", "fsdp"), None), P()
    return jax.shard_map(
        shards,
        mesh=mesh,
        in_specs=(rows,) * 3 + (split,) * 8 + (same,) * 8,
        out_specs=(rows, rows, same, same, same, same),
        check_vma=False,
    )
```

```python
import jax
import jax.numpy as jnp
from jax import lax
from jax.experimental import pallas as pl
from jax.experimental.pallas import tpu as pltpu
from jax.sharding import PartitionSpec as P

MESH = pl.DeviceIdType.MESH
BF = jnp.bfloat16
F32 = jnp.float32


def place():
    dp = lax.axis_index("dp")
    fs = lax.axis_index("fsdp")
    return dict(x=fs % 4, y=(dp // 2) * 2 + (fs // 4) % 2, z=fs // 8, c=dp % 2)


def device(at):
    return ((at["y"] // 2) * 2 + at["c"], at["z"] * 8 + (at["y"] % 2) * 4 + at["x"])


def moved(at, axis, delta):
    size = 2 if axis == "c" else 4
    return {**at, axis: (at[axis] + delta + size) % size}


ORDERS = (("x", "y", "z"), ("y", "z", "x"), ("z", "x", "y"))
PEERS = 23


def near(at):
    for step in range(1, 8):
        x, yl = (at["x"] + step) % 4, (at["y"] + step // 4) % 2
        yield {**at, "x": x, "y": (at["y"] // 2) * 2 + yl}


def across(at):
    for step in range(1, 16):
        yh, c = (at["y"] // 2 + step // 8) % 2, (at["c"] + step // 4) % 2
        yield {**at, "y": yh * 2 + at["y"] % 2, "c": c, "z": (at["z"] + step) % 4}


def peers(at):
    return [*near(at), *across(at), {**at, "y": 3 - at["y"]}]


def enter_signal(at):
    for peer in peers(at):
        pl.semaphore_signal(pltpu.get_barrier_semaphore(), inc=1, device_id=device(peer), device_id_type=MESH)


def region(buf, kind, rot, done, at, low, high):
    every = slice(None)
    x, y, z, c = at["x"], at["y"], at["z"], at["c"]
    yh = every if "y" in done else y // 2
    yl = every if "y" in done else y % 2
    zs = every if "z" in done else z
    col = every if "x" in done else pl.ds(pl.multiple_of(x * 128, 128), 128)
    if kind == "panel":
        return buf.at[low:high, yl, yh, c, zs, rot, :, col]
    col = every if "x" in done else pl.ds(pl.multiple_of((x % 2) * 128, 128), 128)
    xh = every if "x" in done else x // 2
    if kind == "down":
        return buf.at[low:high, yh, c, zs, yl, xh, rot, :, col]
    return buf.at[rot, yh, c, zs, yl, xh, :, col]


class Moves:
    def __init__(self, at, bufs, send, recv):
        self.at, self.bufs, self.send, self.recv = at, bufs, send, recv
        self.slots = {}

    def slot(self, key):
        return self.slots.setdefault(key, len(self.slots))

    def copies(self, group, phase):
        kind, low, high = group
        buf = self.bufs[kind]
        for rot in range(3):
            order = ORDERS[rot]
            axis, done = order[phase], order[:phase]
            for delta in (2, 1, 3):
                k = self.slot((group, phase, rot, delta))
                yield (
                    region(buf, kind, rot, done, self.at, low, high),
                    moved(self.at, axis, delta),
                    region(buf, kind, rot, done, moved(self.at, axis, -delta), low, high),
                    k,
                )

    def sibling(self, group):
        kind, low, high = group
        buf = self.bufs[kind]
        k = self.slot((group, "c"))
        for here in (self.at,):
            other = moved(here, "c", 1)
            if kind == "panel":
                mine, theirs = buf.at[low:high, :, :, here["c"]], buf.at[low:high, :, :, other["c"]]
            elif kind == "up_b":
                mine, theirs = buf.at[:, :, here["c"]], buf.at[:, :, other["c"]]
            else:
                mine, theirs = buf.at[low:high, :, here["c"]], buf.at[low:high, :, other["c"]]
            yield mine, other, theirs, k

    def make(self, what):
        mine, target, theirs, k = what
        return pltpu.make_async_remote_copy(
            src_ref=mine,
            dst_ref=mine,
            send_sem=self.send.at[k],
            recv_sem=self.recv.at[k],
            device_id=device(target),
            device_id_type=MESH,
        )

    def arrival(self, what):
        mine, target, theirs, k = what
        return pltpu.make_async_remote_copy(
            src_ref=theirs,
            dst_ref=theirs,
            send_sem=self.send.at[k],
            recv_sem=self.recv.at[k],
            device_id=device(target),
            device_id_type=MESH,
        )

    def listed(self, group, phase):
        return self.sibling(group) if phase == 3 else self.copies(group, phase)

    def start(self, group, phase):
        for what in self.listed(group, phase):
            self.make(what).start()

    def wait(self, group, phase):
        for what in self.listed(group, phase):
            self.arrival(what).wait_recv()

    def sent(self, group, phase):
        for what in self.listed(group, phase):
            self.make(what).wait_send()


def stage_zero(at, shards, packed, landed, half_d, half_b, both_b, both_d, rows, bufs, send, recv):
    w_query, w_key, w_value, w_out, w_up, w_down, shared_a, shared_b = shards
    kvqo = (w_key, w_value, w_query, w_out)
    x, y, z, c = at["x"], at["y"], at["z"], at["c"]
    mine = (y % 2) * 4 + x

    def pick(ch, yl, dx):
        col = yl * 512 + dx * 128
        if ch == 0:
            return shared_a[:, col : col + 128]
        if ch < 4:
            start = (ch - 1) * 256 + col % 256
            return kvqo[col // 256][:, start : start + 128]
        start = (ch - 4) * 1024 + col
        return w_up[:, start : start + 128]

    for yl in range(2):
        for dx in range(4):
            for ch in range(7):
                packed[yl * 4 + dx, :, ch * 128 : ch * 128 + 128] = pick(ch, yl, dx)
    for odd in range(2):
        for r in range(3):
            tile = slice(r * 256 + odd * 128, r * 256 + odd * 128 + 128)
            both_b[odd, :, r * 128 : r * 128 + 128] = shared_b[:, tile]
            both_d[odd, :, r * 128 : r * 128 + 128] = w_down[:, tile]
    landed[pl.ds(mine, 1)] = packed[pl.ds(mine, 1)]
    pl.semaphore_wait(pltpu.get_barrier_semaphore(), PEERS)
    sends, arrivals = [], []
    for step in range(1, 8):
        dx, dy = step % 4, step // 4
        to = {**at, "x": (x + dx) % 4, "y": (y // 2) * 2 + (y + dy) % 2}
        fro = {**at, "x": (x - dx + 4) % 4, "y": (y // 2) * 2 + (y + dy) % 2}
        to_i, fro_i = (to["y"] % 2) * 4 + to["x"], (fro["y"] % 2) * 4 + fro["x"]
        sends.append(pltpu.make_async_remote_copy(
            src_ref=packed.at[to_i], dst_ref=landed.at[mine], send_sem=send.at[step], recv_sem=recv.at[step],
            device_id=device(to), device_id_type=MESH))
        arrivals.append(pltpu.make_async_remote_copy(
            src_ref=packed.at[to_i], dst_ref=landed.at[fro_i], send_sem=send.at[step], recv_sem=recv.at[step],
            device_id=device(to), device_id_type=MESH))
    other = {**at, "x": x + 1 - 2 * (x % 2)}
    for k, (src, dst) in enumerate(((both_d.at[1 - x % 2], half_d), (both_b.at[1 - x % 2], half_b))):
        sends.append(pltpu.make_async_remote_copy(
            src_ref=src, dst_ref=dst, send_sem=send.at[8 + k], recv_sem=recv.at[8 + k],
            device_id=device(other), device_id_type=MESH))
        arrivals.append(sends[-1])
    for copy in sends:
        copy.start()
    for copy in arrivals:
        copy.wait_recv()
    for i in range(8):
        rows[6 * i : 6 * i + 6, :] = landed[i].astype(F32)
    yh, yl = y // 2, y % 2
    block = rows[...].astype(BF).reshape(3, 16, 896)
    own = pl.ds(pl.multiple_of(x * 128, 128), 128)
    for ch in range(7):
        bufs["panel"][ch, yl, yh, c, z, :, :, own] = block[:, :, ch * 128 : ch * 128 + 128]
    lane = pl.ds(pl.multiple_of((x % 2) * 128, 128), 128)

    def joined(mine_too, got):
        a, b = mine_too.astype(F32), got[...].astype(F32)
        even = x % 2 == 0
        return jnp.concatenate([jnp.where(even, a, b), jnp.where(even, b, a)], axis=0).astype(BF)

    block = joined(both_d[x % 2], half_d).reshape(3, 16, 384)
    for k in range(3):
        bufs["down"][k, yh, c, z, yl, x // 2, :, :, lane] = block[:, :, k * 128 : k * 128 + 128]
    pair = joined(both_b[x % 2], half_b)
    for r in range(3):
        bufs["up_b"][r, yh, c, z, yl, x // 2, :, lane] = pair[:, r * 128 : r * 128 + 128]
    for copy in sends:
        copy.wait_send()


PANEL = (7, 2, 2, 2, 4, 3, 16, 512)
DOWN = (3, 2, 2, 4, 2, 2, 3, 16, 256)
UP_B = (3, 2, 2, 4, 2, 2, 16, 256)


LOG2E = 1.4426950408889634
SCALE_Q = 0.125 * LOG2E
NT = (((1,), (1,)), ((), ()))
TN = (((0,), (0,)), ((), ()))
NN = (((1,), (0,)), ((), ()))
FAR = -1e30
GRADS = ("hid", "slope")


def dot(left, right, dims=NN):
    return lax.dot_general(left, right, dims, preferred_element_type=F32)


def span(start, size):
    return pl.ds(pl.multiple_of(start, size), size)


def panel_of(s, ch, half, cols=slice(None)):
    part = s["panel"][ch, half, :, :, :, :, :, cols]
    return part.reshape(768, part.shape[-1])


def first_half(width=128):
    return lax.broadcasted_iota(jnp.int32, (1, width), 1) < 64


def rank_down(s):
    def half(hb, _):
        cols = span(hb * 512, 512)
        lat = dot(s["x"][...].reshape(1024, 768), panel_of(s, 0, hb))
        s["lat"][:, cols] = lat.astype(BF)
        for slot, name in ((8, "scale_dq"), (20, "scale_dv")):
            s["e"][pl.ds(slot + 2 * hb, 2)] = (lat * s[name][:, cols]).astype(BF).reshape(2, 512, 512)
        return 0

    lax.fori_loop(0, 2, half, 0)


def project_keys(s, r):
    x = s["x"][...].reshape(1024, 768)
    s["qkv"][:, r * 768 : r * 768 + 256] = dot(x, panel_of(s, 1 + r, 0, slice(0, 256))).astype(BF)


def project(s, r):
    cols, base = slice(r * 256, r * 256 + 256), r * 768
    x = s["x"][...].reshape(1024, 768)
    for slot, half, off, scale, kept, at, factor in (
        (20, 0, 256, "scale_bv", "vt", 256, None),
        (8, 1, 0, "scale_bq", "qt", 512, SCALE_Q),
    ):
        low, high = (s["e"][slot + 2 * hb : slot + 2 * hb + 2].reshape(1024, 512) for hb in range(2))
        up = s["up_b"][r].reshape(1024, 256)
        t = dot(low, up[:512]) + dot(high, up[512:])
        s[kept][:, cols] = t.astype(BF)
        full = dot(x, panel_of(s, 1 + r, half, slice(off, off + 256))) + s[scale][:, cols] * t
        s["qkv"][:, base + at : base + at + 256] = (full * factor if factor else full).astype(BF)


def masks(s):
    def micro(m, _):
        pos = lax.broadcasted_iota(jnp.int32, (512, 128), 0)
        lane = lax.broadcasted_iota(jnp.int32, (512, 128), 1) % 64
        end = jnp.int32(0)
        pair = jnp.zeros((512, 128), jnp.int32)
        for p in range(4):
            end = end + s["parts"][m, 0, 2 * p] + s["parts"][m, 0, 2 * p + 1]
            pair = pair + (pos >= end).astype(jnp.int32)
        own = lane == pair
        s["mq"][m] = jnp.where(own, 1.0, 0.0).astype(BF)
        s["mk"][m] = jnp.where(own | (lane >= 8), 0.0, FAR).astype(BF)
        return 0

    lax.fori_loop(0, 2, micro, 0)


def places(r, i):
    m, half = i // 2, i % 2
    base = r * 768 + half * 128
    kvq = [span(base + j * 256, 128) for j in range(3)]
    return m, 2 * r + half, span(m * 512, 512), kvq, span(r * 256 + half * 128, 128)


def scores(s, buf, r, i, h):
    m, _, rows, (kc, _, qc), _ = places(r, i)
    mine = first_half() if h == 0 else ~first_half()
    k = jnp.where(mine, s["qkv"][rows, kc], s["mk"][m])
    q = jnp.where(mine, s["qkv"][rows, qc], s["mq"][m])
    buf[:, :512] = dot(q, k, NT)


def mix(s, buf, r, i, h):
    m, p, rows, (_, vc, _), _ = places(r, i)
    mine = first_half() if h == 0 else ~first_half()
    v = s["qkv"][rows, vc]
    sc = buf[:, :512]
    e = jnp.exp2(sc - jnp.max(sc, axis=1, keepdims=True)).astype(BF)
    s["e"][m * 12 + 2 * p + h] = e
    return dot(e, jnp.where(mine, v, jnp.ones_like(v)))


def attend(s, r):
    s_a, s_b = s["f_a"], s["g_one"].at[0:512, :]
    scores(s, s_a, r, 0, 0)

    def pair(i, _):
        _, _, rows, _, cols = places(r, i)
        scores(s, s_b, r, i, 1)
        o0 = mix(s, s_a, r, i, 0)
        scores(s, s_a, r, jnp.minimum(i + 1, 3), 0)
        o1 = mix(s, s_b, r, i, 1)
        total = pltpu.roll(jnp.where(first_half(), o1, o0), 64, 1)
        inverse = 1.0 / total
        s["inv"][rows, cols] = inverse.astype(BF)
        s["att"][rows, cols] = (jnp.where(first_half(), o0, o1) * inverse).astype(BF)
        return 0

    lax.fori_loop(0, 4, pair, 0, unroll=4)


def mean(v):
    return jnp.mean(v, axis=1, keepdims=True)


def norm(v):
    centred = v - mean(v)
    r = lax.rsqrt(mean(centred * centred) + 1e-05)
    return centred * r, r


def norm_back(hat, r, g):
    return r * (g - mean(g) - hat * mean(g * hat))


def by_rows(fn, size=128):
    for start in range(0, 512, size):
        fn(slice(start, start + size))


def middle(s, m, hooks=None):
    rows = span(m * 512, 512)
    hat, hid, slope = s["f_a"], s["hid"], s["slope"]
    other, low, inv = s["g_one"].at[rows, :], s["ga"].at[rows, :], s["inv"].at[rows, :]
    x, cot = s["x"].at[m], s["cot"].at[m]
    att = s["att"][rows, :]
    for r in range(3):
        hat[:, r * 256 : r * 256 + 256] = dot(att, panel_of(s, 1 + r, 1, slice(256, 512)))

    def norm_one(r):
        n, r1 = norm(x[r, :].astype(F32) + hat[r, :])
        hat[r, :] = n
        low[r, :] = (n * s["gain_one"][...] + s["shift_one"][...]).astype(BF)
        s["r1"][r, :] = r1

    by_rows(norm_one)

    if hooks:
        hooks[0]()
    for t in range(6):
        if hooks and t in hooks[2]:
            hooks[2][t]()
        u = dot(low[...], panel_of(s, 4 + t // 2, t % 2))
        cdf = 0.5 + 0.5 * lax.erf(u * 0.7071067811865476)
        cols = span(t * 512, 512)
        hid[:, cols] = (u * cdf).astype(BF)
        slope[:, cols] = (cdf + (u * 0.3989422804014327) * jnp.exp2(u * (u * (-0.5 * LOG2E)))).astype(BF)
    if hooks:
        hooks[1]()
    for k in range(3):
        other[:, k * 256 : k * 256 + 256] = dot(hid[...], s["down"][k].reshape(3072, 256))

    def norm_two(r):
        n2, r2 = norm(hat[r, :] * s["gain_one"][...] + s["shift_one"][...] + other[r, :])
        x[r, :] = (n2 * s["gain_two"][...] + s["shift_two"][...]).astype(BF)
        g = norm_back(n2, r2, cot[r, :].astype(F32) * s["gain_two"][...])
        other[r, :] = g
        low[r, :] = g.astype(BF)

    by_rows(norm_two)

    def back(t, _):
        cols = span(t * 768, 768)
        g = sum(dot(low[:, k * 256 : k * 256 + 256], s["down"][k, t // 2, t % 2].reshape(768, 256), NT) for k in range(3))
        hid[:, cols] = (g * slope[:, cols].astype(F32)).astype(BF)
        return 0

    lax.fori_loop(0, 4, back, 0, unroll=4)

    other[...] += sum(dot(hid[:, t * 512 : t * 512 + 512], panel_of(s, 4 + t // 2, t % 2), NT) for t in range(6))

    def norm_one_back(r):
        g = norm_back(hat[r, :], s["r1"][r, :], other[r, :] * s["gain_one"][...])
        other[r, :] = g
        low[r, :] = g.astype(BF)

    by_rows(norm_one_back)
    hat[...] = sum(dot(low[:, r * 256 : r * 256 + 256], panel_of(s, 1 + r, 1, slice(256, 512)), NT) for r in range(3))

    def scale_att(r):
        low[r, :] = (hat[r, :] * inv[r, :].astype(F32)).astype(BF)

    by_rows(scale_att)


def attend_back(s):
    def third(r, _):
        for i in range(4):
            m, p, rows, (kc, vc, qc), cols = places(r, i)
            k, v, q = s["qkv"][rows, kc], s["qkv"][rows, vc], s["qkv"][rows, qc]
            ga = s["ga"][rows, cols]
            prod = ga.astype(F32) * s["att"][rows, cols].astype(F32)
            gq = gk = gv = None
            lanes = lax.broadcasted_iota(jnp.int32, (1, 128), 1)
            for h in range(2):
                mine = first_half() if h == 0 else ~first_half()
                delta = -jnp.sum(jnp.where(mine, prod, 0.0), axis=1, keepdims=True)
                high = delta.astype(BF)
                rest = (delta - high.astype(F32)).astype(BF)
                zero = jnp.zeros_like(ga)
                gah = jnp.where(mine, ga, zero)
                aug = jnp.where(mine, ga, jnp.where(lanes % 64 == 0, high, jnp.where(lanes % 64 == 1, rest, zero)))
                gp = dot(aug, jnp.where(mine, v, jnp.ones_like(v)), NT)
                e = s["e"][m * 12 + 2 * p + h]
                gs = (e.astype(F32) * gp).astype(BF)
                gvh = dot(e, gah, TN)
                gqh = dot(gs, jnp.where(mine, k, zero))
                gkh = dot(gs, jnp.where(mine, q, zero), TN)
                gq, gk, gv = (gqh, gkh, gvh) if h == 0 else (gq + gqh, gk + gkh, gv + gvh)
            to = s[GRADS[m]]
            to[:, qc] = (gq * 0.125).astype(BF)
            to[:, kc] = (gk * (1.0 / LOG2E)).astype(BF)
            to[:, vc] = gv.astype(BF)
        return 0

    lax.fori_loop(0, 3, third, 0)


def vera_back(s):
    for base, kept, scale, row, keep in ((512, "qt", "scale_bq", 1, "att"), (256, "vt", "scale_bv", 3, "ga")):
        for r in range(3):
            cols = slice(r * 256, r * 256 + 256)

            total = jnp.zeros((1, 256), F32)
            for m in range(2):
                rows = slice(m * 512, m * 512 + 512)
                g = s[GRADS[m]][:, r * 768 + base : r * 768 + base + 256].astype(F32)
                s[keep][rows, cols] = (g * s[scale][:, cols]).astype(BF)
                total = total + jnp.sum(g * s[kept][rows, cols].astype(F32), axis=0, keepdims=True)
            s["red"][row : row + 1, cols] = total

    def half(hb, _):
        cols = span(hb * 512, 512)
        for m in range(2):
            rows = slice(m * 512, m * 512 + 512)
            gqu, gvu = (
                sum(dot(s[name][rows, r * 256 : r * 256 + 256], s["up_b"][r, hb].reshape(512, 256), NT) for r in range(3))
                for name in ("att", "ga")
            )
            lat = s["lat"][rows, cols].astype(F32)
            for row, val in ((0, gqu), (2, gvu)):
                part = jnp.sum(val * lat, axis=0, keepdims=True)
                if m:
                    part = part + s["red"][row : row + 1, cols]
                s["red"][row : row + 1, cols] = part
            s["e"][2 * hb + m] = (gqu * s["scale_dq"][:, cols] + gvu * s["scale_dv"][:, cols]).astype(BF)
        return 0

    lax.fori_loop(0, 2, half, 0)


def token_grads(s, m):
    rows = slice(m * 512, m * 512 + 512)
    terms = []
    for r in range(3):
        for j, (half, off) in enumerate(((0, 0), (0, 256), (1, 0))):
            lo = r * 768 + j * 256
            terms.append(dot(s[GRADS[m]][:, lo : lo + 256], panel_of(s, 1 + r, half, slice(off, off + 256)), NT))
    for hb in range(2):
        terms.append(dot(s["e"][2 * hb + m], panel_of(s, 0, hb), NT))
    s["cot"][m] = (s["g_one"][rows, :] + sum(terms)).astype(BF)


LAYER_SCRATCH = dict(
    panel=(PANEL, BF),
    down=(DOWN, BF),
    up_b=(UP_B, BF),
    x=((2, 512, 768), BF),
    cot=((2, 512, 768), BF),
    lat=((1024, 1024), BF),
    qt=((1024, 768), BF),
    vt=((1024, 768), BF),
    qkv=((1024, 2304), BF),
    e=((24, 512, 512), BF),
    att=((1024, 768), BF),
    inv=((1024, 768), BF),
    ga=((1024, 768), BF),
    g_one=((1024, 768), F32),
    f_a=((512, 768), F32),
    hid=((512, 3072), BF),
    slope=((512, 3072), BF),
    mq=((2, 512, 128), BF),
    mk=((2, 512, 128), BF),
    r1=((512, 1), F32),
    red=((4, 1024), F32),
)


VECTORS = ("gain_one", "shift_one", "gain_two", "shift_two", "scale_dq", "scale_bq", "scale_dv", "scale_bv")
SHARDS = ("w_query", "w_key", "w_value", "w_out", "w_up", "w_down", "shared_a", "shared_b")
SHARD_SHAPES = ((6, 768),) * 4 + ((6, 3072), (24, 768), (6, 1024), (8, 768))
GROUP_A, GROUP_1, GROUP_2, GROUP_3, UP_0, UP_1, UP_2 = (("panel", i, i + 1) for i in range(7))
DOWN_0, DOWN_1, DOWN_2 = (("down", i, i + 1) for i in range(3))
GROUP_B, FRONT, GROUP_UP, GROUP_DOWN = ("up_b", 0, 3), ("panel", 0, 4), ("panel", 4, 7), ("down", 0, 3)
LATE = (GROUP_UP, GROUP_DOWN)


def near_place(at):
    return (at["y"] % 2) * 4 + at["x"]


def across_place(at):
    return 8 + ((at["y"] // 2) * 2 + at["c"]) * 4 + at["z"]


def reduce_start(at, group, place_of, s, send, recv):
    here = place_of(at)
    s["sums"][pl.ds(here, 1)] = s["red"][...][None]
    sends, arrivals = [], []
    for i, other in enumerate(group(at)):
        k = i if place_of is near_place else 7 + i
        for found, slot in ((sends, here), (arrivals, place_of(other))):
            found.append(pltpu.make_async_remote_copy(
                src_ref=s["sums"].at[here], dst_ref=s["sums"].at[slot],
                send_sem=send.at[k], recv_sem=recv.at[place_of(other)] if found is arrivals else recv.at[here],
                device_id=device(other), device_id_type=MESH))
    for copy in sends:
        copy.start()
    return sends, arrivals


def reduce_end(state, first, size, s):
    sends, arrivals = state
    for copy in arrivals:
        copy.wait_recv()
    for copy in sends:
        copy.wait_send()
    values = [s["sums"][first + i] for i in range(size)]
    while len(values) > 1:
        values = [values[i] + values[i + 1] for i in range(0, len(values), 2)]
    s["red"][...] = values[0]


EXTRA = dict(
    packed=((8, 6, 896), BF),
    landed=((8, 6, 896), BF),
    half_d=((24, 384), BF),
    half_b=((8, 384), BF),
    both_b=((2, 8, 384), BF),
    both_d=((2, 24, 384), BF),
    rows=((48, 896), F32),
    sums=((24, 4, 1024), F32),
)


def whole(*refs):
    names = ("tokens", "parts_in", "cotangent") + tuple("in_" + n for n in SHARDS) + tuple("in_" + n for n in VECTORS)
    names += ("out", "grad_tokens", "grad_dq", "grad_bq", "grad_dv", "grad_bv")
    scratch = tuple(LAYER_SCRATCH) + tuple(EXTRA) + SHARDS + VECTORS
    names += scratch + ("parts", "loads", "send_0", "recv_0", "send", "recv", "send_r", "recv_r")
    s = dict(zip(names, refs, strict=True))
    at = place()
    enter_signal(at)
    loads = []
    pairs = [(s["in_" + n], s[n]) for n in SHARDS] + [(s["in_" + n], s[n].at[0]) for n in VECTORS]
    pairs += [(s["parts_in"], s["parts"]), (s["tokens"], s["x"]), (s["cotangent"], s["cot"])]
    for i, (src, dst) in enumerate(pairs):
        loads.append(pltpu.make_async_copy(src, dst, s["loads"].at[i]))
        loads[-1].start()
    for copy in loads[:8]:
        copy.wait()
    bufs = {k: s[k] for k in ("panel", "down", "up_b")}
    stage_zero(at, [s[n] for n in SHARDS], s["packed"], s["landed"], s["half_d"], s["half_b"], s["both_b"], s["both_d"], s["rows"], bufs, s["send_0"], s["recv_0"])
    moves = Moves(at, bufs, s["send"], s["recv"])
    begun = []

    def start(group, phase):
        moves.start(group, phase)
        begun.append((group, phase))

    def pass_on(group):
        moves.wait(group, 2)
        start(group, 3)

    def before_up():
        for group in (UP_0, UP_1, UP_2):
            moves.wait(group, 3)

    def before_down():
        for group in (DOWN_0, DOWN_1, DOWN_2):
            moves.wait(group, 3)

    hooks = (before_up, before_down, {i + 3: lambda g=g: pass_on(g) for i, g in enumerate((DOWN_0, DOWN_1, DOWN_2))})

    start(FRONT, 0)
    start(GROUP_B, 0)
    moves.wait(FRONT, 0)
    start(FRONT, 1)
    moves.wait(GROUP_B, 0)
    start(GROUP_B, 1)
    for group in LATE:
        start(group, 0)
    moves.wait(FRONT, 1)
    start(GROUP_A, 2)
    start(GROUP_1, 2)
    moves.wait(GROUP_B, 1)
    start(GROUP_B, 2)
    start(GROUP_2, 2)
    for group in LATE:
        moves.wait(group, 0)
        start(group, 1)
    for copy in loads[8:]:
        copy.wait()
    masks(s)
    pass_on(GROUP_A)
    start(GROUP_3, 2)
    moves.wait(GROUP_UP, 1)
    start(UP_0, 2)
    moves.wait(GROUP_A, 3)
    rank_down(s)
    pass_on(GROUP_1)
    pass_on(GROUP_B)
    start(UP_1, 2)
    start(UP_2, 2)
    moves.wait(GROUP_1, 3)
    project_keys(s, 0)
    moves.wait(GROUP_B, 3)
    project(s, 0)
    pass_on(GROUP_2)
    moves.wait(GROUP_DOWN, 1)
    start(DOWN_0, 2)
    attend(s, 0)
    pass_on(GROUP_3)
    start(DOWN_1, 2)
    moves.wait(GROUP_2, 3)
    project_keys(s, 1)
    project(s, 1)
    start(DOWN_2, 2)
    attend(s, 1)
    pass_on(UP_0)
    moves.wait(GROUP_3, 3)
    project_keys(s, 2)
    project(s, 2)
    pass_on(UP_1)
    attend(s, 2)
    pass_on(UP_2)
    middle(s, 0, hooks)
    middle(s, 1)
    result = pltpu.make_async_copy(s["x"], s["out"], s["loads"].at[0])
    result.start()
    for group, phase in begun:
        moves.sent(group, phase)
    attend_back(s)
    vera_back(s)
    for row in (1, 3):
        s["red"][row : row + 1, 768:1024] = jnp.zeros((1, 256), F32)
    state = reduce_start(at, near, near_place, s, s["send_r"], s["recv_r"])
    token_grads(s, 0)
    ends = [result]
    ends.append(pltpu.make_async_copy(s["cot"].at[0], s["grad_tokens"].at[0], s["loads"].at[1]))
    ends[-1].start()
    reduce_end(state, 0, 8, s)
    state = reduce_start(at, across, across_place, s, s["send_r"], s["recv_r"])
    token_grads(s, 1)
    ends.append(pltpu.make_async_copy(s["cot"].at[1], s["grad_tokens"].at[1], s["loads"].at[6]))
    ends[-1].start()
    reduce_end(state, 8, 16, s)
    for i, name in enumerate(("grad_dq", "grad_bq", "grad_dv", "grad_bv")):
        ends.append(pltpu.make_async_copy(s["red"].at[i, 0 : s[name].shape[0]], s[name], s["loads"].at[2 + i]))
        ends[-1].start()
    assert len(moves.slots) == 182
    assert len(moves.slots) == 182
    for copy in ends:
        copy.wait()


def hand_over(*refs):
    sources, results, held, sems = refs[:6], refs[6:12], refs[12:18], refs[18:]
    pieces = []
    for i, (src, dst, mid) in enumerate(zip(sources, results, held, strict=True)):
        if i < 2:
            pieces += [[a.at[m, r : r + 256] for a in (src, mid, dst)] for m in range(2) for r in (0, 256)]
        else:
            pieces.append([src, mid, dst])
    ins = [pltpu.make_async_copy(a, b, sems[0].at[k]) for k, (a, b, _) in enumerate(pieces)]
    outs = [pltpu.make_async_copy(b, c, sems[1].at[k]) for k, (_, b, c) in enumerate(pieces)]
    for copy in ins:
        copy.start()
    for before, after in zip(ins, outs, strict=True):
        before.wait()
        after.start()
    for copy in outs:
        copy.wait()


def shards(tokens, parts, cotangent, *rest):
    anywhere = pl.BlockSpec(memory_space=pl.ANY)
    scratch = [pltpu.VMEM(shape, kind) for shape, kind in (*LAYER_SCRATCH.values(), *EXTRA.values())]
    scratch += [pltpu.VMEM(shape, BF) for shape in SHARD_SHAPES]
    scratch += [pltpu.VMEM((1, v.shape[0]), F32) for v in rest[8:]]
    scratch += [pltpu.SMEM((2, 1, 8), jnp.int32)]
    scratch += [pltpu.SemaphoreType.DMA((n,)) for n in (19, 10, 10, 182, 182, 22, 24)]
    shapes = [jax.ShapeDtypeStruct((2, 512, 768), BF)] * 2
    shapes += [jax.ShapeDtypeStruct((n,), F32) for n in (1024, 768, 1024, 768)]
    found = pl.pallas_call(
        whole,
        out_shape=shapes,
        in_specs=[anywhere] * 19,
        out_specs=[anywhere] * 6,
        scratch_shapes=scratch,
        compiler_params=pltpu.CompilerParams(collective_id=0, has_side_effects=True, vmem_limit_bytes=66900000),
    )(tokens, parts, cotangent, *rest)
    held = [pltpu.VMEM(shape.shape, shape.dtype) for shape in shapes]
    return tuple(pl.pallas_call(
        hand_over,
        out_shape=shapes,
        in_specs=[anywhere] * 6,
        out_specs=[anywhere] * 6,
        scratch_shapes=held + [pltpu.SemaphoreType.DMA((12,))] * 2,
        compiler_params=pltpu.CompilerParams(vmem_limit_bytes=66900000),
    )(*found))


def solution(mesh):
    rows, split, same = P(None, ("dp", "fsdp"), None), P(("dp", "fsdp"), None), P()
    return jax.shard_map(
        shards,
        mesh=mesh,
        in_specs=(rows,) * 3 + (split,) * 8 + (same,) * 8,
        out_specs=(rows, rows, same, same, same, same),
        check_vma=False,
    )
```
